32 devices in a mesh: wide: 16 (over z, y, core), field: 2 (over x).
Axes of the slice: x: 2, y: 2, z: 4, core: 2. Of those that a mesh axis runs over, the one named last changes fastest.
Arguments:
- fine_field_in: bfloat16 [128, 32, 512], P('wide', 'field'), may hold values from -6 to 6
- fine_points: float32 [256, 3, 1024], P(('wide', 'field')), may hold values from -1 to 1
- coarse_points: float32 [256, 3, 1024], P(('wide', 'field')), may hold values from -1 to 1
- quad_weights: float32 [256, 1024], P(('wide', 'field')), may hold values from 0.00390625 to 0.01171875
- pair_fine: int32 [256], P('wide'), may hold values from 0 to 7, as said below
- pair_owner: int32 [256, 1], P('wide'), may hold values from 0 to 15; in each aligned block of 16 rows (0 to 15, 16 to 31, ...) at most 2 rows name the same one
- pair_coarse: int32 [256], P('wide'), may hold values from 0 to 15
- coarse_faces: int32 [256, 6], P('wide'), may hold values from 0 to 255, as said below
- coarse_inv_mass: float32 [256], P('wide'), may hold values from 0.5 to 2
- fine_inv_mass: float32 [128], P('wide'), may hold values from 0.5 to 2
Outputs:
- coarse_field: bfloat16 [256, 32, 512], P('wide', 'field')
- fine_field: bfloat16 [128, 32, 512], P('wide', 'field')
The draws below stay inside these ranges and needn't reach their ends.
Inputs may be any that keep to these rules, and one draw needn't show every extreme that they name: `pair_fine`: within each aligned block of 16 pairs (one partition) every value 0 to 7 appears at least once. `pair_owner`: in each aligned block of 16 rows (one partition) no owner is named more than 2 times, a bound that some block reaches. `coarse_faces`: the owner of a neighbour (index // 16) differs from the element's own owner by at most one; a boundary face names the element itself.
All inputs are finite; a program needn't handle non-finite values.
Results may differ from the reference program's by a relative error of at most 0.007.
Values may be sent and summed in bfloat16 or wider, within the bound.
No kernel may reach another device: no remote copies, remote signals or barrier semaphores. Data moves between devices by JAX's collectives and lax.ppermute only.
A program may use at most 64 MiB of HBM per device.

```python
import math
import jax
import jax.numpy as jnp
import numpy as np
from jax import lax

NB = 8
P_SIZE = 512
QUAD = 1024
CAP = 2
CE_DEV = 16
PAIRS_GRP = 16
FINE_GRP = 8
FIELDS = 32
NPAIR = 256
NFINE = 128
NCOARSE = 256
N_WIDE = 16


def one_group(key):
    first, second = jax.random.split(key)
    extra = jax.random.randint(first, (PAIRS_GRP - FINE_GRP,), 0, FINE_GRP, dtype=jnp.int32)
    base = jnp.concatenate([jnp.arange(FINE_GRP, dtype=jnp.int32), extra])
    return jax.random.permutation(second, base)


def draw_pair_fine(key, part):
    keys = jax.random.split(jax.random.fold_in(key, 11), NPAIR // PAIRS_GRP)
    return jax.vmap(one_group)(keys).reshape(NPAIR).astype(jnp.int32)


def draw_coarse_faces(key, part):
    first, second, third = jax.random.split(jax.random.fold_in(key, 23), 3)
    owners = NCOARSE // CE_DEV
    own = (jnp.arange(NCOARSE, dtype=jnp.int32) // CE_DEV)[:, None]
    step = jax.random.randint(first, (NCOARSE, 6), -1, 2, dtype=jnp.int32)
    other = jnp.clip(own + step, 0, owners - 1)
    local = jax.random.randint(second, (NCOARSE, 6), 0, CE_DEV, dtype=jnp.int32)
    border = jax.random.randint(third, (NCOARSE, 6), 0, 6, dtype=jnp.int32) == 0
    itself = jnp.broadcast_to(jnp.arange(NCOARSE, dtype=jnp.int32)[:, None], (NCOARSE, 6))
    return jnp.where(border, itself, other * CE_DEV + local).astype(jnp.int32)


def touch_ends(values, key, smallest, top_value):
    extent = values.shape
    place = [jax.random.randint(jax.random.fold_in(key, axis), (), 0, extent[axis]) for axis in range(len(extent))]
    values = values.at[tuple(place)].set(smallest)
    longest = extent.index(max(extent))
    place[longest] = (place[longest] + 1) % extent[longest]
    return values.at[tuple(place)].set(top_value)


def block_levels(stream_key, dims, pieces, low, top_value):
    loudness = 1.0
    for dim, parts in pieces:
        draws = jax.random.uniform(jax.random.fold_in(jax.random.fold_in(stream_key, 6), dim), (parts,), jnp.float32, low / len(pieces), top_value / len(pieces))
        loudness = loudness * jnp.repeat(jnp.exp(draws), dims[dim] // parts).reshape((-1,) + (1,) * (len(dims) - 1 - dim))
    return loudness


def routed_block(stream_key, own, number, rows, amount, top, bound, lean):
    sequence = jax.random.permutation(stream_key, amount)
    packed, common = shares(amount, rows * top, bound, lean, True), shares(amount, rows * top, bound, lean, False)
    places = jnp.arange(amount)

    def named(lengths, rotation):
        used = int((lengths > 0).sum())
        fixed = max(1, used // 4)
        passed = fixed + (places - fixed + rotation * (used - fixed)) % max(1, amount - fixed)
        return jnp.zeros((amount,), jnp.int32).at[sequence[jnp.where(places < fixed, places, passed)]].set(jnp.asarray(lengths, jnp.int32))

    lengths = jnp.where(number % 4 == 0, named(packed, number // 4), named(common, number - number // 4 - 1))
    mixed = jax.random.permutation(jax.random.fold_in(own, 3), amount)
    donor, sink = mixed[0:amount // 2 * 2:2], mixed[1:amount // 2 * 2:2]
    slack = jnp.minimum(lengths[donor] - 1, bound - lengths[sink]) // 2
    slack = jnp.where((donor == sequence[0]) | (sink == sequence[0]) | (lengths[sink] == 0), 0, jnp.maximum(slack, 0))
    passed = jax.random.randint(jax.random.fold_in(own, 4), (amount // 2,), 0, 1 << 20) % (slack + 1)
    lengths = lengths.at[donor].add(-passed).at[sink].add(passed)
    labels = jnp.searchsorted(jnp.cumsum(lengths), jnp.arange(rows * top), side="right").astype(jnp.int32)
    listing = labels.reshape(top, rows).T
    listing = listing[jax.random.permutation(jax.random.fold_in(own, 1), rows)]
    rotation = jax.random.randint(jax.random.fold_in(own, 2), (rows, 1), 0, top)
    return jnp.take_along_axis(listing, (jnp.arange(top)[None, :] + rotation) % top, axis=1)


def shares(amount, total, limit, lean, full):
    portions = [(1 << 20) // math.isqrt(rank ** lean) + 1 for rank in range(1, amount + 1)]
    largest = limit if full else min(limit, max(-(-total // amount), total * portions[0] // sum(portions)))
    least = 1 if total - largest >= amount - 1 else 0
    holding, surplus = [largest] + [least] * (amount - 1), total - largest - least * (amount - 1)
    while surplus > 0:
        candidates = [i for i in range(1, amount) if holding[i] < largest] or [i for i in range(1, amount) if holding[i] < limit]
        mass, budget = sum([portions[i] for i in candidates]), surplus
        for i in candidates:
            more = min(limit - holding[i], max(1, budget * portions[i] // mass), surplus)
            holding[i] = holding[i] + more
            surplus = surplus - more
    return np.array(holding)


def scatter_about(key, dims, scale, most, cuts=(), held_as=jnp.bfloat16):
    level = block_levels(key, dims, cuts, -0.22, 0.18) if cuts else 1.0
    array = jax.random.normal(key, dims, jnp.float32) * scale * level
    return jnp.minimum(jnp.maximum(array, -most), most).astype(held_as)


def setup_inputs(seed: int = 0) -> dict:
    splits = jax.random.split(jax.random.key(seed), 11)
    fine_field_in = scatter_about(splits[0], (NFINE, FIELDS, P_SIZE), 1.0, 6.0, ((0, 16), (1, 2)))
    fine_points = jnp.clip(jax.random.uniform(splits[1], (NPAIR, 3, QUAD), jnp.float32, -1.0, 1.0) * block_levels(splits[1], (NPAIR, 3, QUAD), ((0, 32),), -0.4, 0.0), -1.0, 1.0)
    coarse_points = jnp.clip(jax.random.uniform(splits[2], (NPAIR, 3, QUAD), jnp.float32, -1.0, 1.0) * block_levels(splits[2], (NPAIR, 3, QUAD), ((0, 32),), -0.4, 0.0), -1.0, 1.0)
    quad_weights = jnp.clip(0.00390625 + 0.0078125 * jax.random.uniform(splits[3], (NPAIR, QUAD), jnp.float32) ** block_levels(splits[3], (NPAIR, QUAD), ((0, 32),), -0.2, 0.2), 0.00390625, 0.01171875)
    pair_fine = draw_pair_fine(jax.random.fold_in(splits[10], 71), 0)
    pair_owner_keys = jax.random.split(jax.random.fold_in(splits[5], 1), NPAIR // PAIRS_GRP)
    pair_owner_turns = jax.random.permutation(jax.random.fold_in(splits[5], 3), NPAIR // PAIRS_GRP)
    pair_owner = jax.vmap(lambda own, number: routed_block(jax.random.fold_in(splits[5], 2), own, number, PAIRS_GRP, N_WIDE, 1, CAP, 2))(pair_owner_keys, pair_owner_turns).reshape((NPAIR, 1))
    pair_coarse = touch_ends(jax.random.randint(splits[6], (NPAIR,), 0, CE_DEV), jax.random.fold_in(splits[6], 1), 0, CE_DEV - 1).astype(jnp.int32)
    coarse_faces = draw_coarse_faces(jax.random.fold_in(splits[10], 71), 0)
    coarse_inv_mass = jnp.clip(jnp.exp(math.log(2.0) - 1.3862944 * jax.random.uniform(splits[8], (NCOARSE,), jnp.float32) ** block_levels(splits[8], (NCOARSE,), ((0, 16),), -0.2, 0.2)), 0.5, 2.0)
    fine_inv_mass = jnp.clip(jnp.exp(math.log(2.0) - 1.3862944 * jax.random.uniform(splits[9], (NFINE,), jnp.float32) ** block_levels(splits[9], (NFINE,), ((0, 16),), -0.2, 0.2)), 0.5, 2.0)
    return {"fine_field_in": fine_field_in, "fine_points": fine_points, "coarse_points": coarse_points, "quad_weights": quad_weights, "pair_fine": pair_fine, "pair_owner": pair_owner, "pair_coarse": pair_coarse, "coarse_faces": coarse_faces, "coarse_inv_mass": coarse_inv_mass, "fine_inv_mass": fine_inv_mass}


DIFFUSE = 0.125

def legendre(points, count):
    values = [jnp.ones_like(points), points]
    for degree in range(1, count - 1):
        values.append(((2 * degree + 1) * points * values[degree] - degree * values[degree - 1]) / (degree + 1))
    values = values[:count]
    return jnp.stack([values[n] * math.sqrt((2 * n + 1) / 2.0) for n in range(count)])

def basis(points, count):
    table = legendre(points, count)
    product = table[:, None, None, 0, :] * table[None, :, None, 1, :] * table[None, None, :, 2, :]
    return product.reshape(count * count * count, points.shape[-1])

def build_tile(fine_pts, coarse_pts, weights):
    left = (basis(coarse_pts, NB) * weights[None, :]).astype(jnp.bfloat16)
    right = basis(fine_pts, NB).astype(jnp.bfloat16)
    return lax.dot_general(left, right, (((1,), (1,)), ((), ())), preferred_element_type=jnp.float32).astype(jnp.bfloat16)

def reference(fine_field_in, fine_points, coarse_points, quad_weights, pair_fine, pair_owner, pair_coarse, coarse_faces, coarse_inv_mass, fine_inv_mass):
    tiles = lax.map(lambda item: build_tile(item[0], item[1], item[2]), (fine_points, coarse_points, quad_weights))
    npairs = pair_fine.shape[0]
    group = (jnp.arange(npairs, dtype=jnp.int32) // PAIRS_GRP).astype(jnp.int32)
    fine_ids = (group * FINE_GRP + pair_fine).astype(jnp.int32)
    coarse_ids = (pair_owner[:, 0] * CE_DEV + pair_coarse).astype(jnp.int32)

    def add_coarse(total, item):
        tile, fine_id, coarse_id = item
        contrib = lax.dot_general(fine_field_in[fine_id], tile, (((1,), (1,)), ((), ())), preferred_element_type=jnp.float32).astype(jnp.bfloat16)
        return (total.at[coarse_id].add(contrib.astype(jnp.float32)), None)
    start = jnp.zeros((NCOARSE, FIELDS, P_SIZE), jnp.float32)
    load, _ = lax.scan(add_coarse, start, (tiles, fine_ids, coarse_ids))
    solved = coarse_inv_mass[:, None, None] * load
    beside = jnp.zeros_like(solved)
    for face in range(6):
        beside = beside + solved[coarse_faces[:, face]]
    smoothed = solved + DIFFUSE * (beside - 6.0 * solved)
    coarse_field = smoothed.astype(jnp.bfloat16)

    def add_fine(total, item):
        tile, fine_id, coarse_id = item
        term = jnp.dot(coarse_field[coarse_id], tile, preferred_element_type=jnp.float32).astype(jnp.bfloat16)
        return (total.at[fine_id].add(term.astype(jnp.float32)), None)
    start_fine = jnp.zeros((NFINE, FIELDS, P_SIZE), jnp.float32)
    fine_sum, _ = lax.scan(add_fine, start_fine, (tiles, fine_ids, coarse_ids))
    fine_field = (fine_inv_mass[:, None, None] * fine_sum).astype(jnp.bfloat16)
    return (coarse_field, fine_field)
```

```python
import functools
import math

import jax
import jax.numpy as jnp
from jax import lax
from jax.experimental import pallas as pl
from jax.experimental.pallas import tpu as pltpu
from jax.sharding import PartitionSpec as P

NB = 8
DIFFUSE = 0.125
PACK = 16
LANES = 128

NT = (((1,), (1,)), ((), ()))
NN = (((1,), (0,)), ((), ()))


def legendre(points, count):
    values = [jnp.ones_like(points), points]
    for degree in range(1, count - 1):
        values.append(
            ((2 * degree + 1) * points * values[degree] - degree * values[degree - 1])
            / (degree + 1)
        )
    values = values[:count]
    return [values[n] * math.sqrt((2 * n + 1) / 2.0) for n in range(count)]


def fill_table(table_ref, rows_ref, legs, base, here):
    for lane in range(legs.shape[1]):
        cols = slice(lane * LANES, (lane + 1) * LANES)
        first = legs[base, lane, here, :]
        second = legs[base + 1, lane, here, :]
        third = legs[base + 2, lane, here, :]
        for a in range(NB):
            rows_ref[lane, a * NB : (a + 1) * NB, :] = first[a : a + 1, :] * second
        for ab in range(0, NB * NB, 2):
            low = rows_ref[lane, ab : ab + 1, :] * third
            high = rows_ref[lane, ab + 1 : ab + 2, :] * third
            table_ref[ab * NB : (ab + 2) * NB, cols] = jnp.concatenate(
                [low, high], axis=0
            ).astype(jnp.bfloat16)


def project_kernel(fine_ids, points_ref, field_ref, *refs):
    tile_ref, contrib_ref, legs, rows, left, right, sums = refs[-7:]
    pair = pl.program_id(0)
    pairs = points_ref.shape[1]
    block = field_ref.shape[1]

    @pl.when(pair == 0)
    def _():
        for lane in range(legs.shape[1]):
            cols = slice(lane * LANES, (lane + 1) * LANES)
            for coord in range(6):
                values = legendre(points_ref[coord, :, cols], NB)
                for n in range(NB):
                    value = values[n] * points_ref[6, :, cols] if coord == 3 else values[n]
                    legs[coord, lane, pl.ds(n, pairs, stride=NB), :] = value

    here = pl.ds(pl.multiple_of(pair * NB, NB), NB)
    fill_table(right, rows, legs, 0, here)
    fill_table(left, rows, legs, 3, here)
    tile = lax.dot_general(
        left[...], right[...], NT, preferred_element_type=jnp.float32
    ).astype(jnp.bfloat16)
    tile_ref[0] = tile
    contrib = lax.dot_general(
        field_ref[fine_ids[pair]], tile, NT, preferred_element_type=jnp.float32
    )
    for lane in range(sums.shape[0]):
        cols = slice(lane * LANES, (lane + 1) * LANES)
        sums[lane, pl.ds(pair, block, stride=pairs), :] = contrib[:, cols]

    @pl.when(pair == pairs - 1)
    def _():
        for lane in range(sums.shape[0]):
            cols = slice(lane * LANES, (lane + 1) * LANES)
            contrib_ref[:, cols] = sums[lane].astype(jnp.bfloat16)


def project(fine_ids, points, field, tiles, shift, shifts):
    _, pairs, quad = points.shape
    fine_count, block, basis = field.shape
    in_specs = [
        pl.BlockSpec((7, pairs, quad), lambda p, ids: (0, 0, 0)),
        pl.BlockSpec((fine_count, block, basis), lambda p, ids: (0, 0, 0)),
    ]
    operands = [fine_ids, points, field]
    aliases = {}
    if tiles is not None:
        in_specs.append(pl.BlockSpec(memory_space=pl.ANY))
        operands.append(tiles)
        aliases = {3: 0}
    grid_spec = pltpu.PrefetchScalarGridSpec(
        num_scalar_prefetch=1,
        grid=(pairs,),
        in_specs=in_specs,
        out_specs=[
            pl.BlockSpec((1, basis, basis), lambda p, ids: (shift * pairs + p, 0, 0)),
            pl.BlockSpec((block * pairs, basis), lambda p, ids: (0, 0)),
        ],
        scratch_shapes=[
            pltpu.VMEM((6, quad // LANES, pairs * NB, LANES), jnp.float32),
            pltpu.VMEM((quad // LANES, NB * NB, LANES), jnp.float32),
            pltpu.VMEM((basis, quad), jnp.bfloat16),
            pltpu.VMEM((basis, quad), jnp.bfloat16),
            pltpu.VMEM((basis // LANES, block * pairs, LANES), jnp.float32),
        ],
    )
    return pl.pallas_call(
        project_kernel,
        grid_spec=grid_spec,
        out_shape=[
            jax.ShapeDtypeStruct((shifts * pairs, basis, basis), jnp.bfloat16),
            jax.ShapeDtypeStruct((block * pairs, basis), jnp.bfloat16),
        ],
        input_output_aliases=aliases,
        compiler_params=pltpu.CompilerParams(vmem_limit_bytes=32 * 1024 * 1024),
        cost_estimate=pl.CostEstimate(
            flops=2 * pairs * basis * basis * (quad + block),
            bytes_accessed=2 * pairs * basis * basis,
            transcendentals=0,
        ),
        name="project",
    )(*operands)


def combine_kernel(weight_ref, gathered_ref, *refs):
    out_ref = refs[-1]
    weight = weight_ref[...]
    high = weight.astype(jnp.bfloat16)
    low = (weight - high.astype(jnp.float32)).astype(jnp.bfloat16)
    wide, span, basis = gathered_ref.shape
    values = gathered_ref[...].reshape(wide * span, basis)
    total = lax.dot_general(high, values, NN, preferred_element_type=jnp.float32)
    total = total + lax.dot_general(low, values, NN, preferred_element_type=jnp.float32)
    for lane in range(out_ref.shape[0]):
        part = total[:, lane * LANES : (lane + 1) * LANES]
        if len(refs) > 1:
            part = part + refs[0][lane]
        out_ref[lane] = part


def combine(weight, gathered, before):
    wide, rows, basis = gathered.shape
    group, depth = weight.shape
    span = depth // wide
    steps = rows // span
    in_specs = [
        pl.BlockSpec((group, depth), lambda j: (0, 0)),
        pl.BlockSpec((wide, span, basis), lambda j: (0, j, 0)),
    ]
    operands = [weight, gathered]
    if before is not None:
        in_specs.append(pl.BlockSpec((basis // LANES, group, LANES), lambda j: (0, j, 0)))
        operands.append(before)
    return pl.pallas_call(
        combine_kernel,
        grid=(steps,),
        in_specs=in_specs,
        out_specs=pl.BlockSpec((basis // LANES, group, LANES), lambda j: (0, j, 0)),
        out_shape=jax.ShapeDtypeStruct((basis // LANES, steps * group, LANES), jnp.float32),
        compiler_params=pltpu.CompilerParams(vmem_limit_bytes=32 * 1024 * 1024),
        cost_estimate=pl.CostEstimate(
            flops=4 * steps * group * depth * basis,
            bytes_accessed=2 * wide * rows * basis,
            transcendentals=0,
        ),
        name="combine",
    )(*operands)


def restrict_kernel(fine_ids, inverse, smooth_ref, tile_ref, coarse_ref, fine_ref, sums):
    pair = pl.program_id(0)
    coarse_count, block, _ = coarse_ref.shape
    fine_count = fine_ref.shape[0]
    targets = smooth_ref.shape[1] // block

    def picked(target):
        parts = [
            smooth_ref[lane, pl.ds(target, block, stride=targets), :]
            for lane in range(smooth_ref.shape[0])
        ]
        return jnp.concatenate(parts, axis=1).astype(jnp.bfloat16)

    @pl.when(pair == 0)
    def _():
        sums[...] = jnp.zeros_like(sums)
        for c in range(coarse_count):
            coarse_ref[c] = picked(c)

    term = lax.dot_general(picked(coarse_count + pair), tile_ref[0], NN, preferred_element_type=jnp.float32)
    sums[fine_ids[pair]] += term.astype(jnp.bfloat16).astype(jnp.float32)

    @pl.when(pair == pl.num_programs(0) - 1)
    def _():
        for e in range(fine_count):
            fine_ref[e] = (inverse[e] * sums[e]).astype(jnp.bfloat16)


def restrict(fine_ids, inverse, smooth, tiles, coarse_count, block):
    pairs, basis, _ = tiles.shape
    fine_count = inverse.shape[0]
    grid_spec = pltpu.PrefetchScalarGridSpec(
        num_scalar_prefetch=2,
        grid=(pairs,),
        in_specs=[
            pl.BlockSpec(smooth.shape, lambda p, ids, inv: (0, 0, 0)),
            pl.BlockSpec((1, basis, basis), lambda p, ids, inv: (p, 0, 0)),
        ],
        out_specs=[
            pl.BlockSpec((coarse_count, block, basis), lambda p, ids, inv: (0, 0, 0)),
            pl.BlockSpec((fine_count, block, basis), lambda p, ids, inv: (0, 0, 0)),
        ],
        scratch_shapes=[pltpu.VMEM((fine_count, block, basis), jnp.float32)],
    )
    return pl.pallas_call(
        restrict_kernel,
        grid_spec=grid_spec,
        out_shape=[
            jax.ShapeDtypeStruct((coarse_count, block, basis), jnp.bfloat16),
            jax.ShapeDtypeStruct((fine_count, block, basis), jnp.bfloat16),
        ],
        compiler_params=pltpu.CompilerParams(vmem_limit_bytes=32 * 1024 * 1024),
        cost_estimate=pl.CostEstimate(
            flops=2 * pairs * basis * basis * block,
            bytes_accessed=2 * pairs * basis * basis,
            transcendentals=0,
        ),
        name="restrict",
    )(fine_ids, inverse, smooth, tiles)


def shards(
    fine_field_in,
    fine_points,
    coarse_points,
    quad_weights,
    pair_fine,
    pair_owner,
    pair_coarse,
    coarse_faces,
    coarse_inv_mass,
    fine_inv_mass,
):
    nwide = lax.axis_size("wide")
    nfield = lax.axis_size("field")
    wide_index = lax.axis_index("wide")
    field_index = lax.axis_index("field")
    pairs = fine_points.shape[0]
    block = fine_field_in.shape[1]
    coarse_count = coarse_inv_mass.shape[0]
    faces = coarse_faces.shape[1]
    all_coarse = nwide * coarse_count

    own = jnp.concatenate(
        [
            jnp.swapaxes(fine_points, 0, 1),
            jnp.swapaxes(coarse_points, 0, 1),
            quad_weights[None],
        ],
        axis=0,
    )
    points = [own]
    for shift in range(1, nfield):
        perm = [((i + shift) % nfield, i) for i in range(nfield)]
        points.append(lax.ppermute(own, "field", perm))

    def rolled(ids):
        return jnp.roll(ids.reshape(nfield, pairs), -field_index, axis=0)

    fine_ids = rolled(pair_fine)
    coarse_ids = rolled(pair_owner[:, 0] * coarse_count + pair_coarse)
    facts = jnp.concatenate(
        [
            coarse_ids.reshape(-1).astype(jnp.float32),
            coarse_faces.reshape(-1).astype(jnp.float32),
            coarse_inv_mass,
        ]
    )
    facts = lax.all_gather(facts, "wide", axis=0)
    count = nfield * pairs
    every_pair = facts[:, :count].astype(jnp.int32)
    every_face = facts[:, count : count + coarse_count * faces].astype(jnp.int32)
    every_face = every_face.reshape(all_coarse, faces)
    every_mass = facts[:, count + coarse_count * faces :].reshape(all_coarse)

    names = jnp.arange(all_coarse, dtype=jnp.int32)
    pair_mass = jnp.sum(
        jnp.where(every_pair[:, :, None] == names[None, None, :], every_mass[None, None, :], 0.0),
        axis=2,
    )
    pair_faces = jnp.sum(
        jnp.where(
            coarse_ids.reshape(-1)[:, None, None] == names[None, :, None], every_face[None], 0
        ),
        axis=1,
    )
    target = jnp.concatenate([names[:coarse_count] + wide_index * coarse_count, coarse_ids.reshape(-1)])
    target_faces = jnp.concatenate([coarse_faces, pair_faces], axis=0)
    hits = (1.0 - faces * DIFFUSE) * (
        target[:, None, None] == every_pair[None]
    ).astype(jnp.float32)
    for face in range(faces):
        hits = hits + DIFFUSE * (target_faces[:, face, None, None] == every_pair[None]).astype(
            jnp.float32
        )
    weight = hits * pair_mass[None]
    targets = coarse_count + count
    fold = max(1, PACK // pairs)
    weight = weight.reshape(targets, nwide, nfield, pairs)
    same = jnp.eye(fold, dtype=jnp.float32)
    weights = [
        (same[:, None, None, :, None] * weight[None, :, :, shift, None, :]).reshape(
            fold * targets, nwide * fold * pairs
        )
        for shift in range(nfield)
    ]

    tiles = None
    totals = []
    total = None
    for shift in range(nfield):
        tiles, contrib = project(
            fine_ids[shift], points[shift], fine_field_in, tiles, shift, nfield
        )
        if shift >= 2:
            contrib, _ = lax.optimization_barrier((contrib, totals[shift - 2]))
        gathered = lax.all_gather(contrib, "wide", axis=0)
        total = combine(weights[shift], gathered, total)
        totals.append(total)
    return restrict(
        fine_ids.reshape(-1),
        fine_inv_mass,
        total,
        tiles,
        coarse_count,
        block,
    )


def solution(mesh):
    placed = (
        P("wide", "field", None),
        P(("wide", "field"), None, None),
        P(("wide", "field"), None, None),
        P(("wide", "field"), None),
        P("wide"),
        P("wide", None),
        P("wide"),
        P("wide", None),
        P("wide"),
        P("wide"),
    )
    return jax.shard_map(
        shards,
        mesh=mesh,
        in_specs=placed,
        out_specs=(P("wide", "field", None), P("wide", "field", None)),
        check_vma=False,
    )
```

```python
import functools
import math

import jax
import jax.numpy as jnp
from jax import lax
from jax.experimental import pallas as pl
from jax.experimental.pallas import tpu as pltpu
from jax.sharding import PartitionSpec as P

NB = 8
DIFFUSE = 0.125
LANES = 128

NT = (((1,), (1,)), ((), ()))
NN = (((1,), (0,)), ((), ()))
TN = (((0,), (0,)), ((), ()))

SCALAR = pl.BlockSpec(memory_space=pltpu.SMEM)
VECTOR = pl.BlockSpec(memory_space=pltpu.VMEM)


def legendre(points, count):
    values = [jnp.ones_like(points), points]
    for degree in range(1, count - 1):
        values.append(
            ((2 * degree + 1) * points * values[degree] - degree * values[degree - 1])
            / (degree + 1)
        )
    values = values[:count]
    return [values[n] * math.sqrt((2 * n + 1) / 2.0) for n in range(count)]


def lanes(index):
    return slice(index * LANES, (index + 1) * LANES)


def fill_table(table_ref, rows_ref, legs, base, pair):
    here = pl.ds(pl.multiple_of(pair * NB, NB), NB)
    for lane in range(legs.shape[1]):
        first = legs[base, lane, here, :]
        second = legs[base + 1, lane, here, :]
        third = legs[base + 2, lane, here, :]
        for a in range(NB):
            rows_ref[lane, a * NB : (a + 1) * NB, :] = first[a : a + 1, :] * second
        for ab in range(0, NB * NB, 2):
            low = rows_ref[lane, ab : ab + 1, :] * third
            high = rows_ref[lane, ab + 1 : ab + 2, :] * third
            table_ref[ab * NB : (ab + 2) * NB, lanes(lane)] = jnp.concatenate(
                [low, high], axis=0
            ).astype(jnp.bfloat16)


def facts(owner_ref, coarse_ref, faces_ref, inverse_ref, rows, pair_at):
    elements, faces = faces_ref.shape
    lane = lax.broadcasted_iota(jnp.int32, (1, LANES), 1)
    lines = []
    for row in range(rows):
        line = jnp.zeros((1, LANES), jnp.float32)
        if row < coarse_ref.shape[0]:
            pair = pair_at(row)
            line = jnp.where(lane == 0, owner_ref[pair, 0].astype(jnp.float32), line)
            line = jnp.where(lane == 1, coarse_ref[pair].astype(jnp.float32), line)
        if row < elements:
            for face in range(faces):
                name = faces_ref[row, face]
                outer = lax.div(name, jnp.int32(elements))
                inner = name - outer * elements
                line = jnp.where(lane == 2 + 2 * face, outer.astype(jnp.float32), line)
                line = jnp.where(lane == 3 + 2 * face, inner.astype(jnp.float32), line)
            rest = jnp.full((1, LANES), inverse_ref[row], jnp.float32)
            for part in range(3):
                head = rest.astype(jnp.bfloat16).astype(jnp.float32)
                line = jnp.where(lane == 2 + 2 * faces + part, head, line)
                rest = rest - head
        lines.append(line)
    return jnp.concatenate(lines, axis=0).astype(jnp.bfloat16)


def project_kernel(shift, shifts, last, place_ref, fine_ref, *refs):
    if last:
        owner_ref, coarse_ref, faces_ref, inverse_ref = refs[:4]
        refs = refs[4:]
    points_ref, field_ref = refs[:2]
    before = refs[2 : len(refs) - 12]
    tile_ref, out_ref, legs, sums = refs[-12:-8]
    rows, tables = refs[-8:-4], refs[-4:]
    pairs = points_ref.shape[1]
    block = field_ref.shape[1]

    def pair_at(step, pair):
        part = place_ref[0] + step
        return jnp.where(part >= shifts, part - shifts, part) * pairs + pair

    for lane in range(legs.shape[1]):
        for coord in range(6):
            values = legendre(points_ref[coord, :, lanes(lane)], NB)
            for n in range(NB):
                value = values[n] * points_ref[6, :, lanes(lane)] if coord == 3 else values[n]
                legs[coord, lane, pl.ds(n, pairs, stride=NB), :] = value

    def fill(pair, slot):
        fill_table(tables[2 * slot], rows[2 * slot], legs, 0, pair)
        fill_table(tables[2 * slot + 1], rows[2 * slot + 1], legs, 3, pair)

    def apply(pair, slot):
        tile = lax.dot_general(
            tables[2 * slot + 1][...], tables[2 * slot][...], NT, preferred_element_type=jnp.float32
        ).astype(jnp.bfloat16)
        tile_ref[pair] = tile
        contrib = lax.dot_general(
            field_ref[fine_ref[pair_at(shift, pair)]], tile, NT, preferred_element_type=jnp.float32
        )
        for lane in range(sums.shape[0]):
            sums[lane, pl.ds(pair, block, stride=pairs), :] = contrib[:, lanes(lane)]

    fill(0, 0)

    @pl.loop(0, pairs // 2)
    def _(step):
        pair = 2 * step
        fill(pair + 1, 1)
        apply(pair, 0)
        fill(jnp.minimum(pair + 2, pairs - 1), 0)
        apply(pair + 1, 1)

    if not last:
        out_ref[...] = sums[...]
        return
    wide, total, span = out_ref.shape
    width = span - LANES
    across = sums.shape[0]
    extra = facts(
        owner_ref,
        coarse_ref,
        faces_ref,
        inverse_ref,
        total,
        lambda row: pair_at(row // pairs, row % pairs),
    )
    sources = list(before) + [sums]
    for dest in range(wide):
        for piece in range(width // LANES):
            column = dest * (width // LANES) + piece
            row, lane = divmod(column, across)
            parts = [s[lane, row * pairs : (row + 1) * pairs, :] for s in sources]
            out_ref[dest, :, lanes(piece)] = jnp.concatenate(parts, axis=0).astype(jnp.bfloat16)
        out_ref[dest, :, lanes(width // LANES)] = extra


def project(place, fine_ids, scalars, points, field, before, shift, shifts, wide):
    _, pairs, quad = points.shape
    fine_count, block, basis = field.shape
    last = shift == shifts - 1
    across = basis // LANES
    if last:
        out = jax.ShapeDtypeStruct(
            (wide, shifts * pairs, block * basis // wide + LANES), jnp.bfloat16
        )
    else:
        out = jax.ShapeDtypeStruct((across, block * pairs, LANES), jnp.float32)
    operands = [place, fine_ids]
    if last:
        operands += scalars
    specs = [SCALAR] * len(operands)
    vectors = [points, field] + (before if last else [])
    return pl.pallas_call(
        functools.partial(project_kernel, shift, shifts, last),
        in_specs=specs + [VECTOR] * len(vectors),
        out_specs=[VECTOR, VECTOR],
        out_shape=[jax.ShapeDtypeStruct((pairs, basis, basis), jnp.bfloat16), out],
        scratch_shapes=[
            pltpu.VMEM((6, quad // LANES, pairs * NB, LANES), jnp.float32),
            pltpu.VMEM((across, block * pairs, LANES), jnp.float32),
        ]
        + [pltpu.VMEM((quad // LANES, NB * NB, LANES), jnp.float32)] * 4
        + [pltpu.VMEM((basis, quad), jnp.bfloat16)] * 4,
        compiler_params=pltpu.CompilerParams(vmem_limit_bytes=24 * 1024 * 1024),
        cost_estimate=pl.CostEstimate(
            flops=2 * pairs * basis * basis * (quad + block),
            bytes_accessed=2 * pairs * basis * basis,
            transcendentals=0,
        ),
        name="project",
    )(*operands, *vectors)


def coarse_kernel(faces, elements, arrived_ref, out_ref, pick, near, moved):
    wide, rows, span = arrived_ref.shape
    width = span - LANES
    count = wide * elements
    name = lax.broadcasted_iota(jnp.int32, (rows, count), 1).astype(jnp.float32)
    inverse = []
    for source in range(wide):
        fact = arrived_ref[source, :, width:].astype(jnp.float32)
        moved[source * rows : (source + 1) * rows, :] = arrived_ref[source, :, :width]
        index = fact[:, 0:1] * elements + fact[:, 1:2]
        pick[source * rows : (source + 1) * rows, :] = (index == name).astype(jnp.float32).astype(
            jnp.bfloat16
        )
        hits = jnp.zeros((elements, count), jnp.float32)
        for face in range(faces):
            index = fact[:elements, 2 + 2 * face : 3 + 2 * face] * elements
            index = index + fact[:elements, 3 + 2 * face : 4 + 2 * face]
            hits = hits + (index == name[:elements]).astype(jnp.float32)
        near[source * elements : (source + 1) * elements, :] = hits.astype(jnp.bfloat16)
        first = 2 + 2 * faces
        inverse.append(
            fact[:elements, first : first + 1]
            + fact[:elements, first + 1 : first + 2]
            + fact[:elements, first + 2 : first + 3]
        )
    load = lax.dot_general(pick[...], moved[...], TN, preferred_element_type=jnp.float32)
    solved = jnp.concatenate(inverse, axis=0) * load
    high = solved.astype(jnp.bfloat16)
    low = (solved - high.astype(jnp.float32)).astype(jnp.bfloat16)
    beside = lax.dot_general(near[...], high, NN, preferred_element_type=jnp.float32)
    beside = beside + lax.dot_general(near[...], low, NN, preferred_element_type=jnp.float32)
    smooth = (solved + DIFFUSE * (beside - float(faces) * solved)).astype(jnp.bfloat16)
    reply = lax.dot_general(pick[...], smooth, NN, preferred_element_type=jnp.float32).astype(
        jnp.bfloat16
    )
    for dest in range(wide):
        out_ref[dest, :elements, :] = smooth[dest * elements : (dest + 1) * elements, :]
        out_ref[dest, elements:, :] = reply[dest * rows : (dest + 1) * rows, :]


def coarse_stage(arrived, elements, faces):
    wide, rows, span = arrived.shape
    width = span - LANES
    count = wide * elements
    return pl.pallas_call(
        functools.partial(coarse_kernel, faces, elements),
        in_specs=[VECTOR],
        out_specs=VECTOR,
        out_shape=jax.ShapeDtypeStruct((wide, elements + rows, width), jnp.bfloat16),
        scratch_shapes=[
            pltpu.VMEM((wide * rows, count), jnp.bfloat16),
            pltpu.VMEM((count, count), jnp.bfloat16),
            pltpu.VMEM((wide * rows, width), jnp.bfloat16),
        ],
        compiler_params=pltpu.CompilerParams(vmem_limit_bytes=48 * 1024 * 1024),
        cost_estimate=pl.CostEstimate(
            flops=8 * count * wide * rows * width,
            bytes_accessed=4 * wide * rows * width,
            transcendentals=0,
        ),
        name="coarse_stage",
    )(arrived)


def restrict_kernel(shifts, place_ref, fine_ids, inverse_ref, back_ref, *refs):
    tiles = refs[:shifts]
    coarse_ref, fine_ref, rows, sums = refs[shifts:]
    wide, targets, width = back_ref.shape
    elements, block, _ = coarse_ref.shape
    fine_count = fine_ref.shape[0]
    across = rows.shape[0]
    for source in range(wide):
        for piece in range(width // LANES):
            row, lane = divmod(source * (width // LANES) + piece, across)
            rows[lane, row * targets : (row + 1) * targets, :] = back_ref[
                source, :, lanes(piece)
            ].astype(jnp.float32)

    def picked(target):
        parts = [rows[lane, pl.ds(target, block, stride=targets), :] for lane in range(across)]
        return jnp.concatenate(parts, axis=1).astype(jnp.bfloat16)

    sums[...] = jnp.zeros_like(sums)
    for shift in range(shifts):
        part = place_ref[0] + shift
        part = jnp.where(part >= shifts, part - shifts, part)
        pairs = tiles[shift].shape[0]
        for pair in range(pairs):
            term = lax.dot_general(
                picked(elements + shift * pairs + pair),
                tiles[shift][pair],
                NN,
                preferred_element_type=jnp.float32,
            )
            fine = fine_ids[part * pairs + pair]
            sums[fine] += term.astype(jnp.bfloat16).astype(jnp.float32)
    for element in range(elements):
        coarse_ref[element] = picked(element)
    for fine in range(fine_count):
        fine_ref[fine] = (inverse_ref[fine] * sums[fine]).astype(jnp.bfloat16)


def restrict(place, fine_ids, inverse, back, tiles, elements, block):
    pairs, basis, _ = tiles[0].shape
    fine_count = inverse.shape[0]
    targets = back.shape[1]
    return pl.pallas_call(
        functools.partial(restrict_kernel, len(tiles)),
        in_specs=[SCALAR] * 3 + [VECTOR] * (1 + len(tiles)),
        out_specs=[VECTOR, VECTOR],
        out_shape=[
            jax.ShapeDtypeStruct((elements, block, basis), jnp.bfloat16),
            jax.ShapeDtypeStruct((fine_count, block, basis), jnp.bfloat16),
        ],
        scratch_shapes=[
            pltpu.VMEM((basis // LANES, block * targets, LANES), jnp.float32),
            pltpu.VMEM((fine_count, block, basis), jnp.float32),
        ],
        compiler_params=pltpu.CompilerParams(
            vmem_limit_bytes=(16 if len(tiles) <= 2 else 56) * 1024 * 1024
        ),
        cost_estimate=pl.CostEstimate(
            flops=2 * len(tiles) * pairs * basis * basis * block,
            bytes_accessed=2 * len(tiles) * pairs * basis * basis,
            transcendentals=0,
        ),
        name="restrict",
    )(place, fine_ids, inverse, back, *tiles)


def shards(
    fine_field_in,
    fine_points,
    coarse_points,
    quad_weights,
    pair_fine,
    pair_owner,
    pair_coarse,
    coarse_faces,
    coarse_inv_mass,
    fine_inv_mass,
):
    nwide = lax.axis_size("wide")
    nfield = lax.axis_size("field")
    place = lax.axis_index("field").astype(jnp.int32).reshape(1)
    block = fine_field_in.shape[1]
    elements, faces = coarse_faces.shape

    own = jnp.concatenate(
        [
            jnp.swapaxes(fine_points, 0, 1),
            jnp.swapaxes(coarse_points, 0, 1),
            quad_weights[None],
        ],
        axis=0,
    )
    points = [own]
    for shift in range(1, nfield):
        perm = [((i + shift) % nfield, i) for i in range(nfield)]
        points.append(lax.ppermute(own, "field", perm))

    scalars = [pair_owner, pair_coarse, coarse_faces, coarse_inv_mass]
    tiles = []
    outs = []
    for shift in range(nfield):
        tile, out = project(
            place, pair_fine, scalars, points[shift], fine_field_in, outs, shift, nfield, nwide
        )
        tiles.append(tile)
        outs.append(out)
    arrived = lax.all_to_all(outs[-1], "wide", split_axis=0, concat_axis=0, tiled=True)
    smooth = coarse_stage(arrived, elements, faces)
    back = lax.all_to_all(smooth, "wide", split_axis=0, concat_axis=0, tiled=True)
    return restrict(place, pair_fine, fine_inv_mass, back, tiles, elements, block)


def solution(mesh):
    placed = (
        P("wide", "field", None),
        P(("wide", "field"), None, None),
        P(("wide", "field"), None, None),
        P(("wide", "field"), None),
        P("wide"),
        P("wide", None),
        P("wide"),
        P("wide", None),
        P("wide"),
        P("wide"),
    )
    return jax.shard_map(
        shards,
        mesh=mesh,
        in_specs=placed,
        out_specs=(P("wide", "field", None), P("wide", "field", None)),
        check_vma=False,
    )
```

```python
import functools
import math

import jax
import jax.numpy as jnp
from jax import lax
from jax.experimental import pallas as pl
from jax.experimental.pallas import tpu as pltpu
from jax.sharding import PartitionSpec as P

NB = 8
DIFFUSE = 0.125
LANES = 128

NT = (((1,), (1,)), ((), ()))
NN = (((1,), (0,)), ((), ()))
TN = (((0,), (0,)), ((), ()))

SCALAR = pl.BlockSpec(memory_space=pltpu.SMEM)
VECTOR = pl.BlockSpec(memory_space=pltpu.VMEM)
DISTANT = pl.BlockSpec(memory_space=pltpu.HBM)


def legendre(points, count):
    values = [jnp.ones_like(points), points]
    for degree in range(1, count - 1):
        values.append(
            ((2 * degree + 1) * points * values[degree] - degree * values[degree - 1])
            / (degree + 1)
        )
    values = values[:count]
    return [values[n] * math.sqrt((2 * n + 1) / 2.0) for n in range(count)]


def lanes(index):
    return slice(index * LANES, (index + 1) * LANES)


def fill_table(table_ref, legs, base, pair):
    start = pl.multiple_of(pair * NB, NB)
    for lane in range(legs.shape[1]):
        third = legs[base + 2, lane, pl.ds(start, NB), :]
        outer = [legs[base, lane, pl.ds(start + a, 1), :] * third for a in range(NB)]
        inner = [
            jnp.broadcast_to(legs[base + 1, lane, pl.ds(start + b, 1), :], (NB, LANES))
            for b in range(NB)
        ]
        for a in range(NB):
            for b in range(0, NB, 2):
                both = jnp.concatenate([outer[a] * inner[b], outer[a] * inner[b + 1]], axis=0)
                row = (a * NB + b) * NB
                table_ref[row : row + 2 * NB, lanes(lane)] = both.astype(jnp.bfloat16)


def facts(owner_ref, coarse_ref, faces_ref, inverse_ref, rows, pair_at):
    faces, elements = faces_ref.shape
    lane = lax.broadcasted_iota(jnp.int32, (1, LANES), 1)
    lines = []
    for row in range(rows):
        line = jnp.zeros((1, LANES), jnp.float32)
        if row < coarse_ref.shape[0]:
            pair = pair_at(row)
            line = jnp.where(lane == 0, owner_ref[0, pair].astype(jnp.float32), line)
            line = jnp.where(lane == 1, coarse_ref[pair].astype(jnp.float32), line)
        if row < elements:
            for face in range(faces):
                name = faces_ref[face, row]
                outer = lax.div(name, jnp.int32(elements))
                inner = name - outer * elements
                line = jnp.where(lane == 2 + 2 * face, outer.astype(jnp.float32), line)
                line = jnp.where(lane == 3 + 2 * face, inner.astype(jnp.float32), line)
            rest = jnp.full((1, LANES), inverse_ref[row], jnp.float32)
            for part in range(3):
                head = rest.astype(jnp.bfloat16).astype(jnp.float32)
                line = jnp.where(lane == 2 + 2 * faces + part, head, line)
                rest = rest - head
        lines.append(line)
    return jnp.concatenate(lines, axis=0).astype(jnp.bfloat16)


def project_kernel(shift, shifts, last, place_ref, *refs):
    if last:
        owner_ref, coarse_ref, faces_ref, inverse_ref = refs[:4]
        refs = refs[4:]
    points_ref, fine_hbm, field_hbm = refs[:3]
    before = refs[3 : len(refs) - 11]
    tile_ref, out_ref, legs, sums, fine_ref, field_ref, arrive = refs[-11:-4]
    tables = refs[-4:]
    fetches = [
        pltpu.make_async_copy(fine_hbm, fine_ref, arrive.at[0]),
        pltpu.make_async_copy(field_hbm, field_ref, arrive.at[1]),
    ]
    for fetch in fetches:
        fetch.start()
    pairs = points_ref.shape[1]
    block = field_ref.shape[1]

    def pair_at(step, pair):
        part = place_ref[0] + step
        return jnp.where(part >= shifts, part - shifts, part) * pairs + pair

    for lane in range(legs.shape[1]):
        for coord in range(6):
            values = legendre(points_ref[coord, :, lanes(lane)], NB)
            for n in range(NB):
                value = values[n] * points_ref[6, :, lanes(lane)] if coord == 3 else values[n]
                legs[coord, lane, pl.ds(n, pairs, stride=NB), :] = value

    def fill(pair, slot):
        fill_table(tables[2 * slot], legs, 0, pair)
        fill_table(tables[2 * slot + 1], legs, 3, pair)

    def apply(pair, slot):
        tile = lax.dot_general(
            tables[2 * slot + 1][...], tables[2 * slot][...], NT, preferred_element_type=jnp.float32
        ).astype(jnp.bfloat16)
        tile_ref[pair] = tile
        contrib = lax.dot_general(
            field_ref[fine_ref[pair_at(shift, pair)]], tile, NT, preferred_element_type=jnp.float32
        )
        for lane in range(sums.shape[0]):
            sums[lane, pl.ds(pair, block, stride=pairs), :] = contrib[:, lanes(lane)]

    fill(0, 0)
    for fetch in fetches:
        fetch.wait()

    @pl.loop(0, pairs // 2)
    def _(step):
        pair = 2 * step
        fill(pair + 1, 1)
        apply(pair, 0)
        fill(jnp.minimum(pair + 2, pairs - 1), 0)
        apply(pair + 1, 1)

    if not last:
        out_ref[...] = sums[...]
        return
    wide, total, span = out_ref.shape
    width = span - LANES
    across = sums.shape[0]
    extra = facts(
        owner_ref,
        coarse_ref,
        faces_ref,
        inverse_ref,
        total,
        lambda row: pair_at(row // pairs, row % pairs),
    )
    sources = list(before) + [sums]
    for dest in range(wide):
        for piece in range(width // LANES):
            column = dest * (width // LANES) + piece
            row, lane = divmod(column, across)
            parts = [s[lane, row * pairs : (row + 1) * pairs, :] for s in sources]
            out_ref[dest, :, lanes(piece)] = jnp.concatenate(parts, axis=0).astype(jnp.bfloat16)
        out_ref[dest, :, lanes(width // LANES)] = extra


def project(place, fine_ids, scalars, points, field, before, shift, shifts, wide):
    _, pairs, quad = points.shape
    fine_count, block, basis = field.shape
    last = shift == shifts - 1
    across = basis // LANES
    if last:
        out = jax.ShapeDtypeStruct(
            (wide, shifts * pairs, block * basis // wide + LANES), jnp.bfloat16
        )
    else:
        out = jax.ShapeDtypeStruct((across, block * pairs, LANES), jnp.float32)
    operands = [place] + (scalars if last else [])
    specs = [SCALAR] * len(operands) + [VECTOR, DISTANT, DISTANT]
    vectors = before if last else []
    return pl.pallas_call(
        functools.partial(project_kernel, shift, shifts, last),
        in_specs=specs + [VECTOR] * len(vectors),
        out_specs=[VECTOR, VECTOR],
        out_shape=[jax.ShapeDtypeStruct((pairs, basis, basis), jnp.bfloat16), out],
        scratch_shapes=[
            pltpu.VMEM((6, quad // LANES, pairs * NB, LANES), jnp.float32),
            pltpu.VMEM((across, block * pairs, LANES), jnp.float32),
            pltpu.SMEM(fine_ids.shape, jnp.int32),
            pltpu.VMEM(field.shape, field.dtype),
            pltpu.SemaphoreType.DMA((2,)),
        ]
        + [pltpu.VMEM((basis, quad), jnp.bfloat16)] * 4,
        compiler_params=pltpu.CompilerParams(vmem_limit_bytes=24 * 1024 * 1024),
        cost_estimate=pl.CostEstimate(
            flops=2 * pairs * basis * basis * (quad + block),
            bytes_accessed=2 * pairs * basis * basis,
            transcendentals=0,
        ),
        name="project",
    )(*operands, points, fine_ids, field, *vectors)


def coarse_kernel(faces, elements, arrived_ref, out_ref, pick, near, moved):
    wide, rows, span = arrived_ref.shape
    width = span - LANES
    count = wide * elements
    name = lax.broadcasted_iota(jnp.int32, (rows, count), 1).astype(jnp.float32)
    inverse = []
    for source in range(wide):
        fact = arrived_ref[source, :, width:].astype(jnp.float32)
        moved[source * rows : (source + 1) * rows, :] = arrived_ref[source, :, :width]
        index = fact[:, 0:1] * elements + fact[:, 1:2]
        pick[source * rows : (source + 1) * rows, :] = (index == name).astype(jnp.float32).astype(
            jnp.bfloat16
        )
        hits = jnp.zeros((elements, count), jnp.float32)
        for face in range(faces):
            index = fact[:elements, 2 + 2 * face : 3 + 2 * face] * elements
            index = index + fact[:elements, 3 + 2 * face : 4 + 2 * face]
            hits = hits + (index == name[:elements]).astype(jnp.float32)
        near[source * elements : (source + 1) * elements, :] = hits.astype(jnp.bfloat16)
        first = 2 + 2 * faces
        inverse.append(
            fact[:elements, first : first + 1]
            + fact[:elements, first + 1 : first + 2]
            + fact[:elements, first + 2 : first + 3]
        )
    load = lax.dot_general(pick[...], moved[...], TN, preferred_element_type=jnp.float32)
    solved = jnp.concatenate(inverse, axis=0) * load
    high = solved.astype(jnp.bfloat16)
    low = (solved - high.astype(jnp.float32)).astype(jnp.bfloat16)
    beside = lax.dot_general(near[...], high, NN, preferred_element_type=jnp.float32)
    beside = beside + lax.dot_general(near[...], low, NN, preferred_element_type=jnp.float32)
    smooth = (solved + DIFFUSE * (beside - float(faces) * solved)).astype(jnp.bfloat16)
    reply = lax.dot_general(pick[...], smooth, NN, preferred_element_type=jnp.float32).astype(
        jnp.bfloat16
    )
    for dest in range(wide):
        out_ref[dest, :elements, :] = smooth[dest * elements : (dest + 1) * elements, :]
        out_ref[dest, elements:, :] = reply[dest * rows : (dest + 1) * rows, :]


def coarse_stage(arrived, elements, faces):
    wide, rows, span = arrived.shape
    width = span - LANES
    count = wide * elements
    return pl.pallas_call(
        functools.partial(coarse_kernel, faces, elements),
        in_specs=[VECTOR],
        out_specs=VECTOR,
        out_shape=jax.ShapeDtypeStruct((wide, elements + rows, width), jnp.bfloat16),
        scratch_shapes=[
            pltpu.VMEM((wide * rows, count), jnp.bfloat16),
            pltpu.VMEM((count, count), jnp.bfloat16),
            pltpu.VMEM((wide * rows, width), jnp.bfloat16),
        ],
        compiler_params=pltpu.CompilerParams(vmem_limit_bytes=48 * 1024 * 1024),
        cost_estimate=pl.CostEstimate(
            flops=8 * count * wide * rows * width,
            bytes_accessed=4 * wide * rows * width,
            transcendentals=0,
        ),
        name="coarse_stage",
    )(arrived)


def restrict_kernel(shifts, place_ref, fine_ids, inverse_ref, back_ref, *refs):
    tiles = refs[:shifts]
    coarse_ref, fine_ref, rows, sums = refs[shifts:]
    wide, targets, width = back_ref.shape
    elements, block, _ = coarse_ref.shape
    fine_count = fine_ref.shape[0]
    across = rows.shape[0]
    for source in range(wide):
        for piece in range(width // LANES):
            row, lane = divmod(source * (width // LANES) + piece, across)
            rows[lane, row * targets : (row + 1) * targets, :] = back_ref[
                source, :, lanes(piece)
            ].astype(jnp.float32)

    def picked(target):
        parts = [rows[lane, pl.ds(target, block, stride=targets), :] for lane in range(across)]
        return jnp.concatenate(parts, axis=1).astype(jnp.bfloat16)

    sums[...] = jnp.zeros_like(sums)
    for shift in range(shifts):
        part = place_ref[0] + shift
        part = jnp.where(part >= shifts, part - shifts, part)
        pairs = tiles[shift].shape[0]
        for pair in range(pairs):
            term = lax.dot_general(
                picked(elements + shift * pairs + pair),
                tiles[shift][pair],
                NN,
                preferred_element_type=jnp.float32,
            )
            fine = fine_ids[part * pairs + pair]
            sums[fine] += term.astype(jnp.bfloat16).astype(jnp.float32)
    for element in range(elements):
        coarse_ref[element] = picked(element)
    for fine in range(fine_count):
        fine_ref[fine] = (inverse_ref[fine] * sums[fine]).astype(jnp.bfloat16)


def restrict(place, fine_ids, inverse, back, tiles, elements, block):
    pairs, basis, _ = tiles[0].shape
    fine_count = inverse.shape[0]
    targets = back.shape[1]
    return pl.pallas_call(
        functools.partial(restrict_kernel, len(tiles)),
        in_specs=[SCALAR] * 3 + [VECTOR] * (1 + len(tiles)),
        out_specs=[VECTOR, VECTOR],
        out_shape=[
            jax.ShapeDtypeStruct((elements, block, basis), jnp.bfloat16),
            jax.ShapeDtypeStruct((fine_count, block, basis), jnp.bfloat16),
        ],
        scratch_shapes=[
            pltpu.VMEM((basis // LANES, block * targets, LANES), jnp.float32),
            pltpu.VMEM((fine_count, block, basis), jnp.float32),
        ],
        compiler_params=pltpu.CompilerParams(
            vmem_limit_bytes=(16 if len(tiles) <= 2 else 56) * 1024 * 1024
        ),
        cost_estimate=pl.CostEstimate(
            flops=2 * len(tiles) * pairs * basis * basis * block,
            bytes_accessed=2 * len(tiles) * pairs * basis * basis,
            transcendentals=0,
        ),
        name="restrict",
    )(place, fine_ids, inverse, back, *tiles)


def shards(
    fine_field_in,
    fine_points,
    coarse_points,
    quad_weights,
    pair_fine,
    pair_owner,
    pair_coarse,
    coarse_faces,
    coarse_inv_mass,
    fine_inv_mass,
):
    nwide = lax.axis_size("wide")
    nfield = lax.axis_size("field")
    place = lax.axis_index("field").astype(jnp.int32).reshape(1)
    block = fine_field_in.shape[1]
    elements, faces = coarse_faces.shape

    own = jnp.concatenate(
        [
            jnp.swapaxes(fine_points, 0, 1),
            jnp.swapaxes(coarse_points, 0, 1),
            quad_weights[None],
        ],
        axis=0,
    )
    points = [own]
    for shift in range(1, nfield):
        perm = [((i + shift) % nfield, i) for i in range(nfield)]
        points.append(lax.ppermute(own, "field", perm))

    scalars = [pair_owner.T, pair_coarse, coarse_faces.T, coarse_inv_mass]
    tiles = []
    outs = []
    for shift in range(nfield):
        tile, out = project(
            place, pair_fine, scalars, points[shift], fine_field_in, outs, shift, nfield, nwide
        )
        tiles.append(tile)
        outs.append(out)
    arrived = lax.all_to_all(outs[-1], "wide", split_axis=0, concat_axis=0, tiled=True)
    smooth = coarse_stage(arrived, elements, faces)
    back = lax.all_to_all(smooth, "wide", split_axis=0, concat_axis=0, tiled=True)
    return restrict(place, pair_fine, fine_inv_mass, back, tiles, elements, block)


def solution(mesh):
    placed = (
        P("wide", "field", None),
        P(("wide", "field"), None, None),
        P(("wide", "field"), None, None),
        P(("wide", "field"), None),
        P("wide"),
        P("wide", None),
        P("wide"),
        P("wide", None),
        P("wide"),
        P("wide"),
    )
    return jax.shard_map(
        shards,
        mesh=mesh,
        in_specs=placed,
        out_specs=(P("wide", "field", None), P("wide", "field", None)),
        check_vma=False,
    )
```

```python
import functools
import math

import jax
import jax.numpy as jnp
from jax import lax
from jax.experimental import pallas as pl
from jax.experimental.pallas import tpu as pltpu
from jax.sharding import PartitionSpec as P

NB = 8
DIFFUSE = 0.125
LANES = 128
DIGIT = 7

NT = (((1,), (1,)), ((), ()))
NN = (((1,), (0,)), ((), ()))
TN = (((0,), (0,)), ((), ()))

SCALAR = pl.BlockSpec(memory_space=pltpu.SMEM)
VECTOR = pl.BlockSpec(memory_space=pltpu.VMEM)


def legendre(points, count):
    values = [jnp.ones_like(points), points]
    for degree in range(1, count - 1):
        values.append(
            ((2 * degree + 1) / (degree + 1)) * points * values[degree]
            - (degree / (degree + 1)) * values[degree - 1]
        )
    values = values[:count]
    return [values[n] * math.sqrt((2 * n + 1) / 2.0) for n in range(count)]


def lanes(index):
    return slice(index * LANES, (index + 1) * LANES)


def fill_table(table_ref, legs, base, pair, lane):
    start = pl.multiple_of(pair * NB, NB)
    third = legs[base + 2, lane, pl.ds(start, NB), :]
    outer = [legs[base, lane, pl.ds(start + a, 1), :] * third for a in range(NB)]
    inner = [
        jnp.broadcast_to(legs[base + 1, lane, pl.ds(start + b, 1), :], (NB, LANES))
        for b in range(NB)
    ]
    for a in range(NB):
        for b in range(0, NB, 2):
            both = jnp.concatenate([outer[a] * inner[b], outer[a] * inner[b + 1]], axis=0)
            row = (a * NB + b) * NB
            table_ref[row : row + 2 * NB, lanes(lane)] = both.astype(jnp.bfloat16)


def facts(owner_ref, coarse_ref, faces_ref, inverse_ref, rows, pair_at):
    faces, elements = faces_ref.shape
    lane = lax.broadcasted_iota(jnp.int32, (1, LANES), 1)
    lines = []
    for row in range(rows):
        line = jnp.zeros((1, LANES), jnp.float32)
        if row < coarse_ref.shape[0]:
            pair = pair_at(row)
            line = jnp.where(lane == 0, owner_ref[0, pair].astype(jnp.float32), line)
            line = jnp.where(lane == 1, coarse_ref[pair].astype(jnp.float32), line)
        if row < elements:
            for face in range(faces):
                name = faces_ref[face, row]
                outer = lax.shift_right_logical(name, DIGIT)
                inner = name - lax.shift_left(outer, DIGIT)
                line = jnp.where(lane == 2 + 2 * face, outer.astype(jnp.float32), line)
                line = jnp.where(lane == 3 + 2 * face, inner.astype(jnp.float32), line)
            rest = jnp.full((1, LANES), inverse_ref[row], jnp.float32)
            for part in range(3):
                head = rest.astype(jnp.bfloat16).astype(jnp.float32)
                line = jnp.where(lane == 2 + 2 * faces + part, head, line)
                rest = rest - head
        lines.append(line)
    return jnp.concatenate(lines, axis=0).astype(jnp.bfloat16)


def project_kernel(shift, shifts, place_ref, *refs):
    last = shift == shifts - 1
    refs = list(refs)
    points_ref = refs.pop(0)
    if shift or last:
        fine_ref, field_ref = refs.pop(0), refs.pop(0)
    prior = [refs.pop(0)] if shift else []
    if last:
        owner_ref, coarse_ref, faces_ref, inverse_ref = refs[:4]
        before = refs[4 : 4 + max(0, shifts - 2)]
        refs = refs[4 + len(before) :]
    tile_ref = refs.pop(0)
    out_ref = refs.pop(0) if shift or last else None
    legs, sums = refs[:2]
    tables = refs[2:]
    pairs = points_ref.shape[1]
    half = tile_ref.shape[1] // 2
    across = sums.shape[0]

    def pair_at(step, pair):
        part = place_ref[0] + step
        return jnp.where(part >= shifts, part - shifts, part) * pairs + pair

    for lane in range(legs.shape[1]):
        for coord in range(6):
            values = legendre(points_ref[coord, :, lanes(lane)], NB)
            for n in range(NB):
                value = values[n] * points_ref[6, :, lanes(lane)] if coord == 3 else values[n]
                legs[coord, lane, pl.ds(n, pairs, stride=NB), :] = value

    def fills(pair, slot):
        return [
            functools.partial(fill_table, tables[2 * slot + side], legs, 3 * side, pair, lane)
            for lane in range(legs.shape[1])
            for side in range(2)
        ]

    def quarter(pair, slot, up, across):
        rows, columns = slice(up * half, (up + 1) * half), slice(across * half, (across + 1) * half)
        tile_ref[pair, rows, columns] = lax.dot_general(
            tables[2 * slot + 1][rows, :],
            tables[2 * slot][columns, :],
            NT,
            preferred_element_type=jnp.float32,
        ).astype(jnp.bfloat16)

    def contribute(source, step, base, pair):
        field = field_ref[fine_ref[pair_at(step, pair)]]
        block = field.shape[0]
        total = sums.shape[1] // block
        contrib = lax.dot_general(field, source[pair], NT, preferred_element_type=jnp.float32)
        for lane in range(across):
            sums[lane, pl.ds(base + pair, block, stride=total), :] = contrib[:, lanes(lane)]

    def turn(pair, slot):
        following = fills(jnp.minimum(pair + 1, pairs - 1), 1 - slot)
        share = len(following) // 4
        for part in range(4):
            quarter(pair, slot, part % 2, part // 2)
            for fill in following[part * share : (part + 1) * share]:
                fill()
        for source in prior:
            contribute(source, shift - 1, 0, pair)

    for fill in fills(0, 0):
        fill()

    @pl.loop(0, pairs // 2)
    def _(step):
        turn(2 * step, 0)
        turn(2 * step + 1, 1)

    if not last:
        if shift:
            out_ref[...] = sums[...]
        return
    base = pairs if shift else 0
    for pair in range(pairs):
        contribute(tile_ref, shift, base, pair)
    wide, total, span = out_ref.shape
    width = span - LANES
    extra = facts(
        owner_ref,
        coarse_ref,
        faces_ref,
        inverse_ref,
        total,
        lambda row: pair_at(row // pairs, row % pairs),
    )
    held = base + pairs
    for dest in range(wide):
        for piece in range(width // LANES):
            row, lane = divmod(dest * (width // LANES) + piece, across)
            parts = [b[lane, row * pairs : (row + 1) * pairs, :] for b in before]
            parts.append(sums[lane, row * held : (row + 1) * held, :])
            out_ref[dest, :, lanes(piece)] = jnp.concatenate(parts, axis=0).astype(jnp.bfloat16)
        out_ref[dest, :, lanes(width // LANES)] = extra


def project(place, fine_ids, scalars, points, field, prior, before, shift, shifts, wide):
    _, pairs, quad = points.shape
    _, block, basis = field.shape
    last = shift == shifts - 1
    across = basis // LANES
    operands, specs = [place, points], [SCALAR, VECTOR]
    outs = [jax.ShapeDtypeStruct((pairs, basis, basis), jnp.bfloat16)]
    held = pairs
    if shift or last:
        operands += [fine_ids, field]
        specs += [SCALAR, VECTOR]
    if shift:
        operands.append(prior)
        specs.append(VECTOR)
    if last:
        operands += scalars + before
        specs += [SCALAR] * len(scalars) + [VECTOR] * len(before)
        held = pairs * min(2, shifts)
        outs.append(
            jax.ShapeDtypeStruct(
                (wide, shifts * pairs, block * basis // wide + LANES), jnp.bfloat16
            )
        )
    elif shift:
        outs.append(jax.ShapeDtypeStruct((across, block * pairs, LANES), jnp.float32))
    return pl.pallas_call(
        functools.partial(project_kernel, shift, shifts),
        in_specs=specs,
        out_specs=[VECTOR] * len(outs),
        out_shape=outs,
        scratch_shapes=[
            pltpu.VMEM((6, quad // LANES, pairs * NB, LANES), jnp.float32),
            pltpu.VMEM((across, block * held, LANES), jnp.float32),
        ]
        + [pltpu.VMEM((basis, quad), jnp.bfloat16)] * 4,
        compiler_params=pltpu.CompilerParams(vmem_limit_bytes=24 * 1024 * 1024),
        cost_estimate=pl.CostEstimate(
            flops=2 * pairs * basis * basis * (quad + block),
            bytes_accessed=2 * pairs * basis * basis,
            transcendentals=0,
        ),
        name="project",
    )(*operands)


def coarse_kernel(faces, elements, arrived_ref, out_ref, pick, near, moved):
    wide, rows, span = arrived_ref.shape
    width = span - LANES
    count = wide * elements
    name = lax.broadcasted_iota(jnp.int32, (rows, count), 1).astype(jnp.float32)
    inverse = []
    for source in range(wide):
        fact = arrived_ref[source, :, width:].astype(jnp.float32)
        moved[source * rows : (source + 1) * rows, :] = arrived_ref[source, :, :width]
        index = fact[:, 0:1] * elements + fact[:, 1:2]
        pick[source * rows : (source + 1) * rows, :] = (index == name).astype(jnp.float32).astype(
            jnp.bfloat16
        )
        hits = jnp.zeros((elements, count), jnp.float32)
        for face in range(faces):
            index = fact[:elements, 2 + 2 * face : 3 + 2 * face] * float(1 << DIGIT)
            index = index + fact[:elements, 3 + 2 * face : 4 + 2 * face]
            hits = hits + (index == name[:elements]).astype(jnp.float32)
        near[source * elements : (source + 1) * elements, :] = hits.astype(jnp.bfloat16)
        first = 2 + 2 * faces
        inverse.append(
            fact[:elements, first : first + 1]
            + fact[:elements, first + 1 : first + 2]
            + fact[:elements, first + 2 : first + 3]
        )
    load = lax.dot_general(pick[...], moved[...], TN, preferred_element_type=jnp.float32)
    solved = jnp.concatenate(inverse, axis=0) * load
    high = solved.astype(jnp.bfloat16)
    low = (solved - high.astype(jnp.float32)).astype(jnp.bfloat16)
    beside = lax.dot_general(near[...], high, NN, preferred_element_type=jnp.float32)
    beside = beside + lax.dot_general(near[...], low, NN, preferred_element_type=jnp.float32)
    smooth = (solved + DIFFUSE * (beside - float(faces) * solved)).astype(jnp.bfloat16)
    reply = lax.dot_general(pick[...], smooth, NN, preferred_element_type=jnp.float32).astype(
        jnp.bfloat16
    )
    for dest in range(wide):
        out_ref[dest, :elements, :] = smooth[dest * elements : (dest + 1) * elements, :]
        out_ref[dest, elements:, :] = reply[dest * rows : (dest + 1) * rows, :]


def coarse_stage(arrived, elements, faces):
    wide, rows, span = arrived.shape
    width = span - LANES
    count = wide * elements
    return pl.pallas_call(
        functools.partial(coarse_kernel, faces, elements),
        in_specs=[VECTOR],
        out_specs=VECTOR,
        out_shape=jax.ShapeDtypeStruct((wide, elements + rows, width), jnp.bfloat16),
        scratch_shapes=[
            pltpu.VMEM((wide * rows, count), jnp.bfloat16),
            pltpu.VMEM((count, count), jnp.bfloat16),
            pltpu.VMEM((wide * rows, width), jnp.bfloat16),
        ],
        compiler_params=pltpu.CompilerParams(vmem_limit_bytes=48 * 1024 * 1024),
        cost_estimate=pl.CostEstimate(
            flops=8 * count * wide * rows * width,
            bytes_accessed=4 * wide * rows * width,
            transcendentals=0,
        ),
        name="coarse_stage",
    )(arrived)


def restrict_kernel(shifts, place_ref, fine_ids, inverse_ref, back_ref, *refs):
    tiles = refs[:shifts]
    coarse_ref, fine_ref, rows, sums = refs[shifts:]
    wide, targets, width = back_ref.shape
    elements, block, _ = coarse_ref.shape
    fine_count = fine_ref.shape[0]
    across = rows.shape[0]
    for source in range(wide):
        for piece in range(width // LANES):
            row, lane = divmod(source * (width // LANES) + piece, across)
            rows[lane, row * targets : (row + 1) * targets, :] = back_ref[
                source, :, lanes(piece)
            ].astype(jnp.float32)

    def picked(target):
        parts = [rows[lane, pl.ds(target, block, stride=targets), :] for lane in range(across)]
        return jnp.concatenate(parts, axis=1).astype(jnp.bfloat16)

    sums[...] = jnp.zeros_like(sums)
    for shift in range(shifts):
        part = place_ref[0] + shift
        part = jnp.where(part >= shifts, part - shifts, part)
        pairs = tiles[shift].shape[0]
        for pair in range(pairs):
            term = lax.dot_general(
                picked(elements + shift * pairs + pair),
                tiles[shift][pair],
                NN,
                preferred_element_type=jnp.float32,
            )
            fine = fine_ids[part * pairs + pair]
            sums[fine] += term.astype(jnp.bfloat16).astype(jnp.float32)
    for element in range(elements):
        coarse_ref[element] = picked(element)
    for fine in range(fine_count):
        fine_ref[fine] = (inverse_ref[fine] * sums[fine]).astype(jnp.bfloat16)


def restrict(place, fine_ids, inverse, back, tiles, elements, block):
    pairs, basis, _ = tiles[0].shape
    fine_count = inverse.shape[0]
    targets = back.shape[1]
    return pl.pallas_call(
        functools.partial(restrict_kernel, len(tiles)),
        in_specs=[SCALAR] * 3 + [VECTOR] * (1 + len(tiles)),
        out_specs=[VECTOR, VECTOR],
        out_shape=[
            jax.ShapeDtypeStruct((elements, block, basis), jnp.bfloat16),
            jax.ShapeDtypeStruct((fine_count, block, basis), jnp.bfloat16),
        ],
        scratch_shapes=[
            pltpu.VMEM((basis // LANES, block * targets, LANES), jnp.float32),
            pltpu.VMEM((fine_count, block, basis), jnp.float32),
        ],
        compiler_params=pltpu.CompilerParams(
            vmem_limit_bytes=(16 if len(tiles) <= 2 else 56) * 1024 * 1024
        ),
        cost_estimate=pl.CostEstimate(
            flops=2 * len(tiles) * pairs * basis * basis * block,
            bytes_accessed=2 * len(tiles) * pairs * basis * basis,
            transcendentals=0,
        ),
        name="restrict",
    )(place, fine_ids, inverse, back, *tiles)


def shards(
    fine_field_in,
    fine_points,
    coarse_points,
    quad_weights,
    pair_fine,
    pair_owner,
    pair_coarse,
    coarse_faces,
    coarse_inv_mass,
    fine_inv_mass,
):
    nwide = lax.axis_size("wide")
    nfield = lax.axis_size("field")
    place = lax.axis_index("field").astype(jnp.int32).reshape(1)
    block = fine_field_in.shape[1]
    elements, faces = coarse_faces.shape

    own = jnp.concatenate(
        [
            jnp.swapaxes(fine_points, 0, 1),
            jnp.swapaxes(coarse_points, 0, 1),
            quad_weights[None],
        ],
        axis=0,
    )
    points = [own]
    for shift in range(1, nfield):
        perm = [((i + shift) % nfield, i) for i in range(nfield)]
        points.append(lax.ppermute(own, "field", perm))

    scalars = [pair_owner.T, pair_coarse, coarse_faces.T, coarse_inv_mass]
    tiles = []
    outs = []
    for shift in range(nfield):
        tile, *out = project(
            place,
            pair_fine,
            scalars,
            points[shift],
            fine_field_in,
            tiles[-1] if tiles else None,
            outs,
            shift,
            nfield,
            nwide,
        )
        tiles.append(tile)
        outs += out
    arrived = lax.all_to_all(outs[-1], "wide", split_axis=0, concat_axis=0, tiled=True)
    smooth = coarse_stage(arrived, elements, faces)
    back = lax.all_to_all(smooth, "wide", split_axis=0, concat_axis=0, tiled=True)
    return restrict(place, pair_fine, fine_inv_mass, back, tiles, elements, block)


def solution(mesh):
    placed = (
        P("wide", "field", None),
        P(("wide", "field"), None, None),
        P(("wide", "field"), None, None),
        P(("wide", "field"), None),
        P("wide"),
        P("wide", None),
        P("wide"),
        P("wide", None),
        P("wide"),
        P("wide"),
    )
    return jax.shard_map(
        shards,
        mesh=mesh,
        in_specs=placed,
        out_specs=(P("wide", "field", None), P("wide", "field", None)),
        check_vma=False,
    )
```

```python
import functools
import math

import jax
import jax.numpy as jnp
from jax import lax
from jax.experimental import pallas as pl
from jax.experimental.pallas import tpu as pltpu
from jax.sharding import PartitionSpec as P

NB = 8
DIFFUSE = 0.125
LANES = 128
DIGIT = 7

NT = (((1,), (1,)), ((), ()))
NN = (((1,), (0,)), ((), ()))
TN = (((0,), (0,)), ((), ()))

SCALAR = pl.BlockSpec(memory_space=pltpu.SMEM)
VECTOR = pl.BlockSpec(memory_space=pltpu.VMEM)


def legendre(points, count):
    values = [jnp.ones_like(points), points]
    for degree in range(1, count - 1):
        values.append(
            ((2 * degree + 1) / (degree + 1)) * points * values[degree]
            - (degree / (degree + 1)) * values[degree - 1]
        )
    values = values[:count]
    return [values[n] * math.sqrt((2 * n + 1) / 2.0) for n in range(count)]


def lanes(index):
    return slice(index * LANES, (index + 1) * LANES)


def spread(ref, coord, lane, row):
    return jnp.broadcast_to(ref[coord, lane, pl.ds(row, 1), :], (NB, LANES))


def fill_table(table_ref, legs, pair):
    for side in range(2):
        for lane in range(legs.shape[1]):
            third = legs[2 * side + 1, lane, pl.ds(pair * NB, NB), :]
            for b in range(0, NB, 2):
                both = [
                    spread(legs, 2 * side, lane, pair * NB + b + step) * third for step in range(2)
                ]
                table_ref[pair, side, b * NB : (b + 2) * NB, lanes(lane)] = jnp.concatenate(
                    both, axis=0
                ).astype(jnp.bfloat16)


def transfer(coefs, table_ref, heads, pair, row, source):
    block = coefs.shape[0]
    quad = table_ref.shape[3]
    side = lax.broadcasted_iota(jnp.int32, (block, LANES), 1) < NB * NB
    keep = [
        jnp.where(side, 1.0, 0.0).astype(jnp.bfloat16),
        jnp.where(side, 0.0, 1.0).astype(jnp.bfloat16),
    ]
    masked = jnp.concatenate(
        [coefs[:, lanes(a // 2)] * keep[a % 2] for a in range(NB)], axis=0
    )
    total = None
    for start in range(0, quad, 2 * LANES):
        columns = slice(start, start + 2 * LANES)
        inward = table_ref[pair, source, :, columns]
        outward = table_ref[pair, 1 - source, :, columns]
        inner = lax.dot_general(
            masked,
            jnp.concatenate([inward, inward], axis=0),
            NN,
            preferred_element_type=jnp.float32,
        )
        outer = []
        for half in range(2):
            lane = start // LANES + half
            pieces = [[] for _ in range(NB)]
            for low in range(0, block, NB):
                value = None
                for a in range(NB):
                    part = inner[a * block + low : a * block + low + NB, lanes(half)]
                    part = part * spread(heads, source, lane, row + a)
                    value = part if value is None else value + part
                for a in range(NB):
                    pieces[a].append(value * spread(heads, 1 - source, lane, row + a))
            outer.append(jnp.concatenate([p for piece in pieces for p in piece], axis=0))
        part = lax.dot_general(
            jnp.concatenate(outer, axis=1).astype(jnp.bfloat16),
            jnp.concatenate([outward, outward], axis=0),
            NT,
            preferred_element_type=jnp.float32,
        )
        total = part if total is None else total + part
    return [
        jnp.where(side, total[a * block : (a + 1) * block], total[(a + 1) * block : (a + 2) * block])
        for a in range(0, NB, 2)
    ]


def facts(owner_ref, coarse_ref, faces_ref, inverse_ref, rows, pair_at):
    faces, elements = faces_ref.shape
    lane = lax.broadcasted_iota(jnp.int32, (1, LANES), 1)
    lines = []
    for row in range(rows):
        line = jnp.zeros((1, LANES), jnp.float32)
        if row < coarse_ref.shape[0]:
            pair = pair_at(row)
            line = jnp.where(lane == 0, owner_ref[0, pair].astype(jnp.float32), line)
            line = jnp.where(lane == 1, coarse_ref[pair].astype(jnp.float32), line)
        if row < elements:
            for face in range(faces):
                name = faces_ref[face, row]
                outer = lax.shift_right_logical(name, DIGIT)
                inner = name - lax.shift_left(outer, DIGIT)
                line = jnp.where(lane == 2 + 2 * face, outer.astype(jnp.float32), line)
                line = jnp.where(lane == 3 + 2 * face, inner.astype(jnp.float32), line)
            rest = jnp.full((1, LANES), inverse_ref[row], jnp.float32)
            for part in range(3):
                head = rest.astype(jnp.bfloat16).astype(jnp.float32)
                line = jnp.where(lane == 2 + 2 * faces + part, head, line)
                rest = rest - head
        lines.append(line)
    return jnp.concatenate(lines, axis=0).astype(jnp.bfloat16)


def project_kernel(shift, shifts, place_ref, fine_ref, *refs):
    last = shift == shifts - 1
    refs = list(refs)
    if last:
        owner_ref, coarse_ref, faces_ref, inverse_ref = refs[:4]
        refs = refs[4:]
    points_ref, field_ref = refs[:2]
    before = refs[2:-5]
    table_ref, heads, out_ref, legs, sums = refs[-5:]
    pairs = points_ref.shape[1]
    block = field_ref.shape[1]
    across = sums.shape[0]

    def pair_at(step, pair):
        part = place_ref[0] + step
        return jnp.where(part >= shifts, part - shifts, part) * pairs + pair

    for lane in range(legs.shape[1]):
        for coord in range(6):
            side, axis = divmod(coord, 3)
            values = legendre(points_ref[coord, :, lanes(lane)], NB)
            for n in range(NB):
                rows = pl.ds(n, pairs, stride=NB)
                if axis:
                    legs[2 * side + axis - 1, lane, rows, :] = values[n]
                elif side:
                    heads[side, lane, rows, :] = values[n] * points_ref[6, :, lanes(lane)]
                else:
                    heads[side, lane, rows, :] = values[n]

    for pair in range(pairs):
        fill_table(table_ref, legs, pair)
        coefs = field_ref[fine_ref[pair_at(shift, pair)]]
        parts = transfer(coefs, table_ref, heads, pair, pair * NB, 0)
        for lane in range(across):
            sums[lane, pl.ds(pair, block, stride=pairs), :] = parts[lane]

    if not last:
        out_ref[...] = sums[...]
        return
    wide, total, span = out_ref.shape
    width = span - LANES
    extra = facts(
        owner_ref,
        coarse_ref,
        faces_ref,
        inverse_ref,
        total,
        lambda row: pair_at(row // pairs, row % pairs),
    )
    sources = list(before) + [sums]
    for dest in range(wide):
        for piece in range(width // LANES):
            row, lane = divmod(dest * (width // LANES) + piece, across)
            parts = [s[lane, row * pairs : (row + 1) * pairs, :] for s in sources]
            out_ref[dest, :, lanes(piece)] = jnp.concatenate(parts, axis=0).astype(jnp.bfloat16)
        out_ref[dest, :, lanes(width // LANES)] = extra


def project(place, fine_ids, scalars, points, field, before, shift, shifts, wide):
    _, pairs, quad = points.shape
    _, block, basis = field.shape
    last = shift == shifts - 1
    across = basis // LANES
    operands = [place, fine_ids] + (scalars if last else [])
    vectors = [points, field] + (before if last else [])
    if last:
        out = jax.ShapeDtypeStruct(
            (wide, shifts * pairs, block * basis // wide + LANES), jnp.bfloat16
        )
    else:
        out = jax.ShapeDtypeStruct((across, block * pairs, LANES), jnp.float32)
    return pl.pallas_call(
        functools.partial(project_kernel, shift, shifts),
        in_specs=[SCALAR] * len(operands) + [VECTOR] * len(vectors),
        out_specs=[VECTOR] * 3,
        out_shape=[
            jax.ShapeDtypeStruct((pairs, 2, NB * NB, quad), jnp.bfloat16),
            jax.ShapeDtypeStruct((2, quad // LANES, pairs * NB, LANES), jnp.float32),
            out,
        ],
        scratch_shapes=[
            pltpu.VMEM((4, quad // LANES, pairs * NB, LANES), jnp.float32),
            pltpu.VMEM((across, block * pairs, LANES), jnp.float32),
        ],
        compiler_params=pltpu.CompilerParams(vmem_limit_bytes=24 * 1024 * 1024),
        cost_estimate=pl.CostEstimate(
            flops=4 * pairs * NB * block * LANES * quad,
            bytes_accessed=2 * pairs * NB * NB * quad,
            transcendentals=0,
        ),
        name="project",
    )(*operands, *vectors)


def coarse_kernel(faces, elements, arrived_ref, out_ref, pick, near, moved):
    wide, rows, span = arrived_ref.shape
    width = span - LANES
    count = wide * elements
    name = lax.broadcasted_iota(jnp.int32, (rows, count), 1).astype(jnp.float32)
    inverse = []
    for source in range(wide):
        fact = arrived_ref[source, :, width:].astype(jnp.float32)
        moved[source * rows : (source + 1) * rows, :] = arrived_ref[source, :, :width]
        index = fact[:, 0:1] * elements + fact[:, 1:2]
        pick[source * rows : (source + 1) * rows, :] = (index == name).astype(jnp.float32).astype(
            jnp.bfloat16
        )
        hits = jnp.zeros((elements, count), jnp.float32)
        for face in range(faces):
            index = fact[:elements, 2 + 2 * face : 3 + 2 * face] * float(1 << DIGIT)
            index = index + fact[:elements, 3 + 2 * face : 4 + 2 * face]
            hits = hits + (index == name[:elements]).astype(jnp.float32)
        near[source * elements : (source + 1) * elements, :] = hits.astype(jnp.bfloat16)
        first = 2 + 2 * faces
        inverse.append(
            fact[:elements, first : first + 1]
            + fact[:elements, first + 1 : first + 2]
            + fact[:elements, first + 2 : first + 3]
        )
    load = lax.dot_general(pick[...], moved[...], TN, preferred_element_type=jnp.float32)
    solved = jnp.concatenate(inverse, axis=0) * load
    high = solved.astype(jnp.bfloat16)
    low = (solved - high.astype(jnp.float32)).astype(jnp.bfloat16)
    beside = lax.dot_general(near[...], high, NN, preferred_element_type=jnp.float32)
    beside = beside + lax.dot_general(near[...], low, NN, preferred_element_type=jnp.float32)
    smooth = (solved + DIFFUSE * (beside - float(faces) * solved)).astype(jnp.bfloat16)
    reply = lax.dot_general(pick[...], smooth, NN, preferred_element_type=jnp.float32).astype(
        jnp.bfloat16
    )
    for dest in range(wide):
        out_ref[dest, :elements, :] = smooth[dest * elements : (dest + 1) * elements, :]
        out_ref[dest, elements:, :] = reply[dest * rows : (dest + 1) * rows, :]


def coarse_stage(arrived, elements, faces):
    wide, rows, span = arrived.shape
    width = span - LANES
    count = wide * elements
    return pl.pallas_call(
        functools.partial(coarse_kernel, faces, elements),
        in_specs=[VECTOR],
        out_specs=VECTOR,
        out_shape=jax.ShapeDtypeStruct((wide, elements + rows, width), jnp.bfloat16),
        scratch_shapes=[
            pltpu.VMEM((wide * rows, count), jnp.bfloat16),
            pltpu.VMEM((count, count), jnp.bfloat16),
            pltpu.VMEM((wide * rows, width), jnp.bfloat16),
        ],
        compiler_params=pltpu.CompilerParams(vmem_limit_bytes=48 * 1024 * 1024),
        cost_estimate=pl.CostEstimate(
            flops=8 * count * wide * rows * width,
            bytes_accessed=4 * wide * rows * width,
            transcendentals=0,
        ),
        name="coarse_stage",
    )(arrived)


def restrict_kernel(shifts, place_ref, fine_ids, inverse_ref, back_ref, *refs):
    tables, heads = refs[:shifts], refs[shifts : 2 * shifts]
    coarse_ref, fine_ref, rows, sums = refs[2 * shifts :]
    wide, targets, width = back_ref.shape
    elements, block, _ = coarse_ref.shape
    fine_count = fine_ref.shape[0]
    across = rows.shape[0]
    for source in range(wide):
        for piece in range(width // LANES):
            row, lane = divmod(source * (width // LANES) + piece, across)
            rows[lane, row * targets : (row + 1) * targets, :] = back_ref[
                source, :, lanes(piece)
            ].astype(jnp.float32)

    def picked(target):
        parts = [rows[lane, pl.ds(target, block, stride=targets), :] for lane in range(across)]
        return jnp.concatenate(parts, axis=1).astype(jnp.bfloat16)

    sums[...] = jnp.zeros_like(sums)
    for shift in range(shifts):
        part = place_ref[0] + shift
        part = jnp.where(part >= shifts, part - shifts, part)
        pairs = tables[shift].shape[0]

        def turn(pair):
            start = pair * NB
            if not isinstance(pair, int):
                start = pl.multiple_of(start, NB)
            coefs = picked(elements + shift * pairs + pair)
            parts = transfer(coefs, tables[shift], heads[shift], pair, start, 1)
            fine = fine_ids[part * pairs + pair]
            for lane in range(across):
                sums[fine, :, lanes(lane)] += parts[lane].astype(jnp.bfloat16).astype(jnp.float32)

        if shifts <= 2:
            for pair in range(pairs):
                turn(pair)
        else:
            pl.loop(0, pairs)(turn)
    for element in range(elements):
        coarse_ref[element] = picked(element)
    for fine in range(fine_count):
        fine_ref[fine] = (inverse_ref[fine] * sums[fine]).astype(jnp.bfloat16)


def restrict(place, fine_ids, inverse, back, tables, heads, elements, block):
    pairs, _, _, quad = tables[0].shape
    fine_count = inverse.shape[0]
    targets = back.shape[1]
    basis = NB * NB * NB
    return pl.pallas_call(
        functools.partial(restrict_kernel, len(tables)),
        in_specs=[SCALAR] * 3 + [VECTOR] * (1 + 2 * len(tables)),
        out_specs=[VECTOR, VECTOR],
        out_shape=[
            jax.ShapeDtypeStruct((elements, block, basis), jnp.bfloat16),
            jax.ShapeDtypeStruct((fine_count, block, basis), jnp.bfloat16),
        ],
        scratch_shapes=[
            pltpu.VMEM((basis // LANES, block * targets, LANES), jnp.float32),
            pltpu.VMEM((fine_count, block, basis), jnp.float32),
        ],
        compiler_params=pltpu.CompilerParams(
            vmem_limit_bytes=(24 if len(tables) <= 2 else 56) * 1024 * 1024
        ),
        cost_estimate=pl.CostEstimate(
            flops=4 * len(tables) * pairs * NB * block * LANES * quad,
            bytes_accessed=2 * len(tables) * pairs * NB * NB * quad,
            transcendentals=0,
        ),
        name="restrict",
    )(place, fine_ids, inverse, back, *tables, *heads)


def shards(
    fine_field_in,
    fine_points,
    coarse_points,
    quad_weights,
    pair_fine,
    pair_owner,
    pair_coarse,
    coarse_faces,
    coarse_inv_mass,
    fine_inv_mass,
):
    nwide = lax.axis_size("wide")
    nfield = lax.axis_size("field")
    place = lax.axis_index("field").astype(jnp.int32).reshape(1)
    block = fine_field_in.shape[1]
    elements, faces = coarse_faces.shape

    own = jnp.concatenate(
        [
            jnp.swapaxes(fine_points, 0, 1),
            jnp.swapaxes(coarse_points, 0, 1),
            quad_weights[None],
        ],
        axis=0,
    )
    points = [own]
    for shift in range(1, nfield):
        perm = [((i + shift) % nfield, i) for i in range(nfield)]
        points.append(lax.ppermute(own, "field", perm))

    scalars = [pair_owner.T, pair_coarse, coarse_faces.T, coarse_inv_mass]
    tables, heads, outs = [], [], []
    for shift in range(nfield):
        table, head, out = project(
            place, pair_fine, scalars, points[shift], fine_field_in, outs, shift, nfield, nwide
        )
        tables.append(table)
        heads.append(head)
        outs.append(out)
    arrived = lax.all_to_all(outs[-1], "wide", split_axis=0, concat_axis=0, tiled=True)
    smooth = coarse_stage(arrived, elements, faces)
    back = lax.all_to_all(smooth, "wide", split_axis=0, concat_axis=0, tiled=True)
    return restrict(place, pair_fine, fine_inv_mass, back, tables, heads, elements, block)


def solution(mesh):
    placed = (
        P("wide", "field", None),
        P(("wide", "field"), None, None),
        P(("wide", "field"), None, None),
        P(("wide", "field"), None),
        P("wide"),
        P("wide", None),
        P("wide"),
        P("wide", None),
        P("wide"),
        P("wide"),
    )
    return jax.shard_map(
        shards,
        mesh=mesh,
        in_specs=placed,
        out_specs=(P("wide", "field", None), P("wide", "field", None)),
        check_vma=False,
    )
```

```python
import functools
import math

import jax
import jax.numpy as jnp
from jax import lax
from jax.experimental import pallas as pl
from jax.experimental.pallas import tpu as pltpu
from jax.sharding import PartitionSpec as P

NB = 8
DIFFUSE = 0.125
LANES = 128
DIGIT = 7
PACK = 16

NT = (((1,), (1,)), ((), ()))
NN = (((1,), (0,)), ((), ()))
TN = (((0,), (0,)), ((), ()))

SCALAR = pl.BlockSpec(memory_space=pltpu.SMEM)
VECTOR = pl.BlockSpec(memory_space=pltpu.VMEM)


def legendre(points, count):
    values = [jnp.ones_like(points), points]
    for degree in range(1, count - 1):
        values.append(
            ((2 * degree + 1) / (degree + 1)) * points * values[degree]
            - (degree / (degree + 1)) * values[degree - 1]
        )
    values = values[:count]
    return [values[n] * math.sqrt((2 * n + 1) / 2.0) for n in range(count)]


def lanes(index):
    return slice(index * LANES, (index + 1) * LANES)


def spread(ref, coord, lane, row):
    return jnp.broadcast_to(ref[coord, lane, pl.ds(row, 1), :], (NB, LANES))


def fill_table(table_ref, legs, pair):
    for side in range(2):
        for lane in range(legs.shape[1]):
            third = legs[2 * side + 1, lane, pl.ds(pair * NB, NB), :]
            for b in range(0, NB, 2):
                both = [
                    spread(legs, 2 * side, lane, pair * NB + b + step) * third for step in range(2)
                ]
                table_ref[pair, side, b * NB : (b + 2) * NB, lanes(lane)] = jnp.concatenate(
                    both, axis=0
                ).astype(jnp.bfloat16)


def transfer(coefs, table_ref, heads, pair, row, source):
    block = coefs.shape[0]
    quad = table_ref.shape[3]
    side = lax.broadcasted_iota(jnp.int32, (block, LANES), 1) < NB * NB
    keep = [
        jnp.where(side, 1.0, 0.0).astype(jnp.bfloat16),
        jnp.where(side, 0.0, 1.0).astype(jnp.bfloat16),
    ]
    masked = jnp.concatenate(
        [coefs[:, lanes(a // 2)] * keep[a % 2] for a in range(NB)], axis=0
    )
    total = None
    for start in range(0, quad, 2 * LANES):
        columns = slice(start, start + 2 * LANES)
        inward = table_ref[pair, source, :, columns]
        outward = table_ref[pair, 1 - source, :, columns]
        inner = lax.dot_general(
            masked,
            jnp.concatenate([inward, inward], axis=0),
            NN,
            preferred_element_type=jnp.float32,
        )
        outer = []
        for half in range(2):
            lane = start // LANES + half
            pieces = [[] for _ in range(NB)]
            for low in range(0, block, NB):
                value = None
                for a in range(NB):
                    part = inner[a * block + low : a * block + low + NB, lanes(half)]
                    part = part * spread(heads, source, lane, row + a)
                    value = part if value is None else value + part
                for a in range(NB):
                    pieces[a].append(value * spread(heads, 1 - source, lane, row + a))
            outer.append(jnp.concatenate([p for piece in pieces for p in piece], axis=0))
        part = lax.dot_general(
            jnp.concatenate(outer, axis=1).astype(jnp.bfloat16),
            jnp.concatenate([outward, outward], axis=0),
            NT,
            preferred_element_type=jnp.float32,
        )
        total = part if total is None else total + part
    return [
        jnp.where(side, total[a * block : (a + 1) * block], total[(a + 1) * block : (a + 2) * block])
        for a in range(0, NB, 2)
    ]


def facts(given_ref, total, elements, faces, rows, pair_at):
    lane = lax.broadcasted_iota(jnp.int32, (1, LANES), 1)
    lines = []
    for row in rows:
        pair = pair_at(row)
        line = jnp.where(lane == 0, given_ref[total + pair], 0.0)
        line = jnp.where(lane == 1, given_ref[2 * total + pair], line)
        if row < elements:
            for face in range(faces):
                name = given_ref[3 * total + face * elements + row].astype(jnp.int32)
                outer = lax.shift_right_logical(name, DIGIT)
                inner = name - lax.shift_left(outer, DIGIT)
                line = jnp.where(lane == 2 + 2 * face, outer.astype(jnp.float32), line)
                line = jnp.where(lane == 3 + 2 * face, inner.astype(jnp.float32), line)
            rest = jnp.full(
                (1, LANES), given_ref[3 * total + faces * elements + row], jnp.float32
            )
            for part in range(3):
                head = rest.astype(jnp.bfloat16).astype(jnp.float32)
                line = jnp.where(lane == 2 + 2 * faces + part, head, line)
                rest = rest - head
        lines.append(line)
    return jnp.concatenate(lines, axis=0).astype(jnp.bfloat16)


def project_kernel(
    shift,
    shifts,
    fold,
    width,
    elements,
    faces,
    place_ref,
    given_ref,
    points_ref,
    field_ref,
    table_ref,
    heads,
    out_ref,
    legs,
    sums,
):
    pairs = points_ref.shape[1]
    block = field_ref.shape[1]
    across = sums.shape[0]

    def pair_at(step, pair):
        part = place_ref[0] + step
        return jnp.where(part >= shifts, part - shifts, part) * pairs + pair

    for lane in range(legs.shape[1]):
        for coord in range(6):
            side, axis = divmod(coord, 3)
            values = legendre(points_ref[coord, :, lanes(lane)], NB)
            for n in range(NB):
                rows = pl.ds(n, pairs, stride=NB)
                if axis:
                    legs[2 * side + axis - 1, lane, rows, :] = values[n]
                elif side:
                    heads[side, lane, rows, :] = values[n] * points_ref[6, :, lanes(lane)]
                else:
                    heads[side, lane, rows, :] = values[n]

    for pair in range(pairs):
        fill_table(table_ref, legs, pair)
        coefs = field_ref[given_ref[pair_at(shift, pair)].astype(jnp.int32)]
        parts = transfer(coefs, table_ref, heads, pair, pair * NB, 0)
        for lane in range(across):
            sums[lane, pl.ds(pair, block, stride=pairs), :] = parts[lane]

    wide = out_ref.shape[0]
    pieces = width // LANES
    slices = block * across // pieces
    for part in range(slices):
        for piece in range(pieces // fold):
            stack = []
            for turn in range(fold):
                row, lane = divmod(part * pieces + turn * (pieces // fold) + piece, across)
                stack.append(sums[lane, row * pairs : (row + 1) * pairs, :])
            value = jnp.concatenate(stack, axis=0).astype(jnp.bfloat16)
            for dest in range(part, wide, slices):
                out_ref[dest, :, lanes(piece)] = value
    if shift == 0:
        span = fold * pairs
        for group in range(shifts // fold):
            extra = facts(
                given_ref,
                shifts * pairs,
                elements,
                faces,
                range(group * span, (group + 1) * span),
                lambda row: pair_at(row // pairs, row % pairs),
            )
            for dest in range(wide):
                out_ref[dest, :, lanes(pieces // fold + group)] = extra


def project(place, given, points, field, shift, shifts, wide, fold, width, elements, faces):
    _, pairs, quad = points.shape
    _, block, basis = field.shape
    across = basis // LANES
    first = shift == 0
    span = width // fold + (shifts // fold * LANES if first else 0)
    return pl.pallas_call(
        functools.partial(project_kernel, shift, shifts, fold, width, elements, faces),
        in_specs=[SCALAR] * 2 + [VECTOR] * 2,
        out_specs=[VECTOR] * 3,
        out_shape=[
            jax.ShapeDtypeStruct((pairs, 2, NB * NB, quad), jnp.bfloat16),
            jax.ShapeDtypeStruct((2, quad // LANES, pairs * NB, LANES), jnp.float32),
            jax.ShapeDtypeStruct((wide, fold * pairs, span), jnp.bfloat16),
        ],
        scratch_shapes=[
            pltpu.VMEM((4, quad // LANES, pairs * NB, LANES), jnp.float32),
            pltpu.VMEM((across, block * pairs, LANES), jnp.float32),
        ],
        compiler_params=pltpu.CompilerParams(vmem_limit_bytes=24 * 1024 * 1024),
        cost_estimate=pl.CostEstimate(
            flops=4 * pairs * NB * block * LANES * quad,
            bytes_accessed=2 * pairs * NB * NB * quad,
            transcendentals=0,
        ),
        name="project",
    )(place, given, points, field)


def plan_kernel(faces, elements, start, arrived_ref, pick, near, inverse):
    wide, _, span = arrived_ref.shape
    rows, count = pick.shape[0] // wide, pick.shape[1]
    name = lax.broadcasted_iota(jnp.int32, (rows, count), 1).astype(jnp.float32)
    for source in range(wide):
        groups = [
            arrived_ref[source, :, column : column + LANES].astype(jnp.float32)
            for column in range(start, span, LANES)
        ]
        fact = jnp.concatenate(groups, axis=0)
        index = fact[:, 0:1] * elements + fact[:, 1:2]
        pick[source * rows : (source + 1) * rows, :] = (index == name).astype(jnp.float32).astype(
            jnp.bfloat16
        )
        fact = fact[:elements]
        hits = jnp.zeros((elements, count), jnp.float32)
        for face in range(faces):
            index = fact[:, 2 + 2 * face : 3 + 2 * face] * float(1 << DIGIT)
            index = index + fact[:, 3 + 2 * face : 4 + 2 * face]
            hits = hits + (index == name[:elements]).astype(jnp.float32)
        here = slice(source * elements, (source + 1) * elements)
        near[here, :] = hits.astype(jnp.bfloat16)
        first = 2 + 2 * faces
        value = (
            fact[:, first : first + 1]
            + fact[:, first + 1 : first + 2]
            + fact[:, first + 2 : first + 3]
        )
        inverse[here, :] = jnp.broadcast_to(value, (elements, LANES))


def plan(arrived, elements, faces, rows, start):
    wide = arrived.shape[0]
    count = wide * elements
    return pl.pallas_call(
        functools.partial(plan_kernel, faces, elements, start),
        in_specs=[VECTOR],
        out_specs=[VECTOR] * 3,
        out_shape=[
            jax.ShapeDtypeStruct((wide * rows, count), jnp.bfloat16),
            jax.ShapeDtypeStruct((count, count), jnp.bfloat16),
            jax.ShapeDtypeStruct((count, LANES), jnp.float32),
        ],
        compiler_params=pltpu.CompilerParams(vmem_limit_bytes=24 * 1024 * 1024),
        cost_estimate=pl.CostEstimate(
            flops=16 * count * count, bytes_accessed=4 * count * count, transcendentals=0
        ),
        name="plan",
    )(arrived)


def coarse_kernel(
    faces, elements, shifts, half_ref, pick, near, inverse_ref, *refs
):
    arrived = refs[:shifts]
    out_ref, moved = refs[shifts:]
    slices, _, width = out_ref.shape
    wide, depth, part = arrived[-1].shape
    fold = width // part
    pairs = depth // fold
    rows = shifts * pairs
    for source in range(wide):
        values = [a[source, :, :part].astype(jnp.float32) for a in arrived]
        for turn in range(fold):
            stack = [v[turn * pairs : (turn + 1) * pairs] for v in values]
            moved[source * rows : (source + 1) * rows, turn * part : (turn + 1) * part] = (
                jnp.concatenate(stack, axis=0).astype(jnp.bfloat16)
            )
    load = lax.dot_general(pick[...], moved[...], TN, preferred_element_type=jnp.float32)
    solved = inverse_ref[:, 0:1] * load
    high = solved.astype(jnp.bfloat16)
    low = (solved - high.astype(jnp.float32)).astype(jnp.bfloat16)
    beside = lax.dot_general(near[...], high, NN, preferred_element_type=jnp.float32)
    beside = beside + lax.dot_general(near[...], low, NN, preferred_element_type=jnp.float32)
    smooth = (solved + DIFFUSE * (beside - float(faces) * solved)).astype(jnp.bfloat16)
    moved_rows = slices * rows
    mine = pl.ds(pl.multiple_of(half_ref[0] * moved_rows, moved_rows), moved_rows)
    reply = lax.dot_general(
        pick[mine, :], smooth, NN, preferred_element_type=jnp.float32
    ).astype(jnp.bfloat16)
    for dest in range(slices):
        out_ref[dest, elements:, :] = reply[dest * rows : (dest + 1) * rows, :]
    held = slices * elements
    for half in range(wide // slices):

        @pl.when(half_ref[0] == half)
        def _():
            for dest in range(slices):
                start = half * held + dest * elements
                out_ref[dest, :elements, :] = smooth[start : start + elements, :]


def coarse_stage(half, pick, near, inverse, arrived, elements, faces, slices, width):
    total, count = pick.shape
    wide = arrived[0].shape[0]
    return pl.pallas_call(
        functools.partial(coarse_kernel, faces, elements, len(arrived)),
        in_specs=[SCALAR] + [VECTOR] * (3 + len(arrived)),
        out_specs=VECTOR,
        out_shape=jax.ShapeDtypeStruct((slices, elements + total // wide, width), jnp.bfloat16),
        scratch_shapes=[pltpu.VMEM((total, width), jnp.bfloat16)],
        compiler_params=pltpu.CompilerParams(vmem_limit_bytes=40 * 1024 * 1024),
        cost_estimate=pl.CostEstimate(
            flops=8 * count * total * width,
            bytes_accessed=4 * total * width,
            transcendentals=0,
        ),
        name="coarse_stage",
    )(half, pick, near, inverse, *arrived)


def restrict_kernel(shifts, place_ref, fine_ids, inverse_ref, back_ref, *refs):
    tables, heads = refs[:shifts], refs[shifts : 2 * shifts]
    coarse_ref, fine_ref, rows, sums = refs[2 * shifts :]
    wide, targets, width = back_ref.shape
    elements, block, _ = coarse_ref.shape
    fine_count = fine_ref.shape[0]
    across = rows.shape[0]
    for source in range(wide):
        for piece in range(width // LANES):
            row, lane = divmod(source * (width // LANES) + piece, across)
            rows[lane, row * targets : (row + 1) * targets, :] = back_ref[
                source, :, lanes(piece)
            ].astype(jnp.float32)

    def picked(target):
        parts = [rows[lane, pl.ds(target, block, stride=targets), :] for lane in range(across)]
        return jnp.concatenate(parts, axis=1).astype(jnp.bfloat16)

    sums[...] = jnp.zeros_like(sums)
    for shift in range(shifts):
        part = place_ref[0] + shift
        part = jnp.where(part >= shifts, part - shifts, part)
        pairs = tables[shift].shape[0]

        def turn(pair):
            start = pair * NB
            if not isinstance(pair, int):
                start = pl.multiple_of(start, NB)
            coefs = picked(elements + shift * pairs + pair)
            parts = transfer(coefs, tables[shift], heads[shift], pair, start, 1)
            fine = fine_ids[part * pairs + pair]
            for lane in range(across):
                sums[fine, :, lanes(lane)] += parts[lane].astype(jnp.bfloat16).astype(jnp.float32)

        if shifts <= 2:
            for pair in range(pairs):
                turn(pair)
        else:
            pl.loop(0, pairs)(turn)
    for element in range(elements):
        coarse_ref[element] = picked(element)
    for fine in range(fine_count):
        fine_ref[fine] = (inverse_ref[fine] * sums[fine]).astype(jnp.bfloat16)


def restrict(place, fine_ids, inverse, back, tables, heads, elements, block):
    pairs, _, _, quad = tables[0].shape
    fine_count = inverse.shape[0]
    targets = back.shape[1]
    basis = NB * NB * NB
    return pl.pallas_call(
        functools.partial(restrict_kernel, len(tables)),
        in_specs=[SCALAR] * 3 + [VECTOR] * (1 + 2 * len(tables)),
        out_specs=[VECTOR, VECTOR],
        out_shape=[
            jax.ShapeDtypeStruct((elements, block, basis), jnp.bfloat16),
            jax.ShapeDtypeStruct((fine_count, block, basis), jnp.bfloat16),
        ],
        scratch_shapes=[
            pltpu.VMEM((basis // LANES, block * targets, LANES), jnp.float32),
            pltpu.VMEM((fine_count, block, basis), jnp.float32),
        ],
        compiler_params=pltpu.CompilerParams(
            vmem_limit_bytes=(24 if len(tables) <= 2 else 56) * 1024 * 1024
        ),
        cost_estimate=pl.CostEstimate(
            flops=4 * len(tables) * pairs * NB * block * LANES * quad,
            bytes_accessed=2 * len(tables) * pairs * NB * NB * quad,
            transcendentals=0,
        ),
        name="restrict",
    )(place, fine_ids, inverse, back, *tables, *heads)


def shards(
    fine_field_in,
    fine_points,
    coarse_points,
    quad_weights,
    pair_fine,
    pair_owner,
    pair_coarse,
    coarse_faces,
    coarse_inv_mass,
    fine_inv_mass,
):
    nwide = lax.axis_size("wide")
    nfield = lax.axis_size("field")
    place = lax.axis_index("field").astype(jnp.int32).reshape(1)
    block = fine_field_in.shape[1]
    elements, faces = coarse_faces.shape

    own = jnp.concatenate(
        [
            jnp.swapaxes(fine_points, 0, 1),
            jnp.swapaxes(coarse_points, 0, 1),
            quad_weights[None],
        ],
        axis=0,
    )
    points = [own]
    for shift in range(1, nfield):
        perm = [((i + shift) % nfield, i) for i in range(nfield)]
        points.append(lax.ppermute(own, "field", perm))

    given = [pair_fine, pair_owner.reshape(-1), pair_coarse, coarse_faces.T.reshape(-1)]
    given = jnp.concatenate([g.astype(jnp.float32) for g in given] + [coarse_inv_mass])
    halves = 2 if nwide % 2 == 0 else 1
    slices = nwide // halves
    width = block * fine_field_in.shape[2] // slices
    pairs = fine_points.shape[0]
    fold = max(1, PACK // pairs)
    if width % (fold * LANES) or nfield % fold:
        fold = 1
    half = (lax.axis_index("wide") // slices).astype(jnp.int32).reshape(1)

    tables, heads, arrived = [], [], []
    for shift in range(nfield):
        table, head, out = project(
            place,
            given,
            points[shift],
            fine_field_in,
            shift,
            nfield,
            nwide,
            fold,
            width,
            elements,
            faces,
        )
        tables.append(table)
        heads.append(head)
        arrived.append(lax.all_to_all(out, "wide", split_axis=0, concat_axis=0, tiled=True))
    pick, near, inverse = plan(arrived[0], elements, faces, nfield * pairs, width // fold)
    smooth = coarse_stage(half, pick, near, inverse, arrived, elements, faces, slices, width)
    groups = [list(range(first, first + slices)) for first in range(0, nwide, slices)]
    back = lax.all_to_all(
        smooth, "wide", split_axis=0, concat_axis=0, axis_index_groups=groups, tiled=True
    )
    return restrict(place, pair_fine, fine_inv_mass, back, tables, heads, elements, block)


def solution(mesh):
    placed = (
        P("wide", "field", None),
        P(("wide", "field"), None, None),
        P(("wide", "field"), None, None),
        P(("wide", "field"), None),
        P("wide"),
        P("wide", None),
        P("wide"),
        P("wide", None),
        P("wide"),
        P("wide"),
    )
    return jax.shard_map(
        shards,
        mesh=mesh,
        in_specs=placed,
        out_specs=(P("wide", "field", None), P("wide", "field", None)),
        check_vma=False,
    )
```

```python
import functools
import math

import jax
import jax.numpy as jnp
from jax import lax
from jax.experimental import pallas as pl
from jax.experimental.pallas import tpu as pltpu
from jax.sharding import PartitionSpec as P

NB = 8
DIFFUSE = 0.125
LANES = 128
DIGIT = 7

NT = (((1,), (1,)), ((), ()))
NN = (((1,), (0,)), ((), ()))
TN = (((0,), (0,)), ((), ()))

SCALAR = pl.BlockSpec(memory_space=pltpu.SMEM)
VECTOR = pl.BlockSpec(memory_space=pltpu.VMEM)


def legendre(points, count):
    values = [jnp.ones_like(points), points]
    for degree in range(1, count - 1):
        values.append(
            ((2 * degree + 1) / (degree + 1)) * points * values[degree]
            - (degree / (degree + 1)) * values[degree - 1]
        )
    values = values[:count]
    return [values[n] * math.sqrt((2 * n + 1) / 2.0) for n in range(count)]


def lanes(index):
    return slice(index * LANES, (index + 1) * LANES)


def spread(ref, coord, lane, row):
    return jnp.broadcast_to(ref[coord, lane, pl.ds(row, 1), :], (NB, LANES))


def fill_table(table_ref, legs, pair):
    for side in range(2):
        for lane in range(legs.shape[1]):
            third = legs[2 * side + 1, lane, pl.ds(pair * NB, NB), :]
            for b in range(0, NB, 2):
                both = [
                    spread(legs, 2 * side, lane, pair * NB + b + step) * third for step in range(2)
                ]
                table_ref[pair, side, b * NB : (b + 2) * NB, lanes(lane)] = jnp.concatenate(
                    both, axis=0
                ).astype(jnp.bfloat16)


def transfer(coefs, table_ref, heads, pair, row, source):
    block = coefs.shape[0]
    quad = table_ref.shape[3]
    pieces = []
    for lane in range(coefs.shape[1] // LANES):
        piece = coefs[:, lanes(lane)]
        pieces += [piece, pltpu.roll(piece, NB * NB, axis=1)]
    packed = jnp.concatenate(pieces, axis=0).astype(jnp.bfloat16)[:, : NB * NB]
    total = None
    for start in range(0, quad, 2 * LANES):
        columns = slice(start, start + 2 * LANES)
        inward = table_ref[pair, source, :, columns]
        outward = table_ref[pair, 1 - source, :, columns]
        inner = lax.dot_general(
            packed,
            inward,
            NN,
            preferred_element_type=jnp.float32,
        )
        outer = []
        for half in range(2):
            lane = start // LANES + half
            pieces = [[] for _ in range(NB)]
            for low in range(0, block, NB):
                value = None
                for a in range(NB):
                    part = inner[a * block + low : a * block + low + NB, lanes(half)]
                    part = part * spread(heads, source, lane, row + a)
                    value = part if value is None else value + part
                for a in range(NB):
                    pieces[a].append(value * spread(heads, 1 - source, lane, row + a))
            outer.append(jnp.concatenate([p for piece in pieces for p in piece], axis=0))
        part = lax.dot_general(
            jnp.concatenate(outer, axis=1).astype(jnp.bfloat16),
            outward,
            NT,
            preferred_element_type=jnp.float32,
        )
        total = part if total is None else total + part
    parts = [total[a * block : (a + 1) * block] for a in range(NB)]
    return [jnp.concatenate(parts[a : a + 2], axis=1) for a in range(0, NB, 2)]


def facts(owner_ref, coarse_ref, faces_ref, inverse_ref, rows, pair_at):
    faces, elements = faces_ref.shape
    lane = lax.broadcasted_iota(jnp.int32, (1, LANES), 1)
    lines = []
    for row in range(rows):
        line = jnp.zeros((1, LANES), jnp.float32)
        if row < coarse_ref.shape[0]:
            pair = pair_at(row)
            line = jnp.where(lane == 0, owner_ref[0, pair].astype(jnp.float32), line)
            line = jnp.where(lane == 1, coarse_ref[pair].astype(jnp.float32), line)
        if row < elements:
            for face in range(faces):
                name = faces_ref[face, row]
                outer = lax.shift_right_logical(name, DIGIT)
                inner = name - lax.shift_left(outer, DIGIT)
                line = jnp.where(lane == 2 + 2 * face, outer.astype(jnp.float32), line)
                line = jnp.where(lane == 3 + 2 * face, inner.astype(jnp.float32), line)
            rest = jnp.full((1, LANES), inverse_ref[row], jnp.float32)
            for part in range(3):
                head = rest.astype(jnp.bfloat16).astype(jnp.float32)
                line = jnp.where(lane == 2 + 2 * faces + part, head, line)
                rest = rest - head
        lines.append(line)
    return jnp.concatenate(lines, axis=0).astype(jnp.bfloat16)


def project_kernel(shift, shifts, place_ref, fine_ref, *refs):
    last = shift == shifts - 1
    refs = list(refs)
    if last:
        owner_ref, coarse_ref, faces_ref, inverse_ref = refs[:4]
        refs = refs[4:]
    points_ref, field_ref = refs[:2]
    before = refs[2:-5]
    table_ref, heads, out_ref, legs, sums = refs[-5:]
    pairs = points_ref.shape[1]
    block = field_ref.shape[1]
    across = sums.shape[0]

    def pair_at(step, pair):
        part = place_ref[0] + step
        return jnp.where(part >= shifts, part - shifts, part) * pairs + pair

    for lane in range(legs.shape[1]):
        for coord in range(6):
            side, axis = divmod(coord, 3)
            values = legendre(points_ref[coord, :, lanes(lane)], NB)
            for n in range(NB):
                rows = pl.ds(n, pairs, stride=NB)
                if axis:
                    legs[2 * side + axis - 1, lane, rows, :] = values[n]
                elif side:
                    heads[side, lane, rows, :] = values[n] * points_ref[6, :, lanes(lane)]
                else:
                    heads[side, lane, rows, :] = values[n]

    for pair in range(pairs):
        fill_table(table_ref, legs, pair)
        coefs = field_ref[fine_ref[pair_at(shift, pair)]].astype(jnp.float32)
        parts = transfer(coefs, table_ref, heads, pair, pair * NB, 0)
        for lane in range(across):
            sums[lane, pl.ds(pair, block, stride=pairs), :] = parts[lane]

    if not last:
        out_ref[...] = sums[...]
        return
    wide, total, span = out_ref.shape
    width = span - LANES
    extra = facts(
        owner_ref,
        coarse_ref,
        faces_ref,
        inverse_ref,
        total,
        lambda row: pair_at(row // pairs, row % pairs),
    )
    sources = list(before) + [sums]
    for dest in range(wide):
        for piece in range(width // LANES):
            row, lane = divmod(dest * (width // LANES) + piece, across)
            parts = [s[lane, row * pairs : (row + 1) * pairs, :] for s in sources]
            out_ref[dest, :, lanes(piece)] = jnp.concatenate(parts, axis=0).astype(jnp.bfloat16)
        out_ref[dest, :, lanes(width // LANES)] = extra


def project(place, fine_ids, scalars, points, field, before, shift, shifts, wide):
    _, pairs, quad = points.shape
    _, block, basis = field.shape
    last = shift == shifts - 1
    across = basis // LANES
    operands = [place, fine_ids] + (scalars if last else [])
    vectors = [points, field] + (before if last else [])
    if last:
        out = jax.ShapeDtypeStruct(
            (wide, shifts * pairs, block * basis // wide + LANES), jnp.bfloat16
        )
    else:
        out = jax.ShapeDtypeStruct((across, block * pairs, LANES), jnp.float32)
    return pl.pallas_call(
        functools.partial(project_kernel, shift, shifts),
        in_specs=[SCALAR] * len(operands) + [VECTOR] * len(vectors),
        out_specs=[VECTOR] * 3,
        out_shape=[
            jax.ShapeDtypeStruct((pairs, 2, NB * NB, quad), jnp.bfloat16),
            jax.ShapeDtypeStruct((2, quad // LANES, pairs * NB, LANES), jnp.float32),
            out,
        ],
        scratch_shapes=[
            pltpu.VMEM((4, quad // LANES, pairs * NB, LANES), jnp.float32),
            pltpu.VMEM((across, block * pairs, LANES), jnp.float32),
        ],
        compiler_params=pltpu.CompilerParams(vmem_limit_bytes=24 * 1024 * 1024),
        cost_estimate=pl.CostEstimate(
            flops=4 * pairs * NB * block * LANES * quad,
            bytes_accessed=2 * pairs * NB * NB * quad,
            transcendentals=0,
        ),
        name="project",
    )(*operands, *vectors)


def coarse_kernel(faces, elements, arrived_ref, out_ref, pick, near, moved):
    wide, rows, span = arrived_ref.shape
    width = span - LANES
    count = wide * elements
    name = lax.broadcasted_iota(jnp.int32, (rows, count), 1).astype(jnp.float32)
    inverse = []
    for source in range(wide):
        fact = arrived_ref[source, :, width:].astype(jnp.float32)
        moved[source * rows : (source + 1) * rows, :] = arrived_ref[source, :, :width]
        index = fact[:, 0:1] * elements + fact[:, 1:2]
        pick[source * rows : (source + 1) * rows, :] = (index == name).astype(jnp.float32).astype(
            jnp.bfloat16
        )
        hits = jnp.zeros((elements, count), jnp.float32)
        for face in range(faces):
            index = fact[:elements, 2 + 2 * face : 3 + 2 * face] * float(1 << DIGIT)
            index = index + fact[:elements, 3 + 2 * face : 4 + 2 * face]
            hits = hits + (index == name[:elements]).astype(jnp.float32)
        near[source * elements : (source + 1) * elements, :] = hits.astype(jnp.bfloat16)
        first = 2 + 2 * faces
        inverse.append(
            fact[:elements, first : first + 1]
            + fact[:elements, first + 1 : first + 2]
            + fact[:elements, first + 2 : first + 3]
        )
    load = lax.dot_general(pick[...], moved[...], TN, preferred_element_type=jnp.float32)
    solved = jnp.concatenate(inverse, axis=0) * load
    high = solved.astype(jnp.bfloat16)
    low = (solved - high.astype(jnp.float32)).astype(jnp.bfloat16)
    beside = lax.dot_general(near[...], high, NN, preferred_element_type=jnp.float32)
    beside = beside + lax.dot_general(near[...], low, NN, preferred_element_type=jnp.float32)
    smooth = (solved + DIFFUSE * (beside - float(faces) * solved)).astype(jnp.bfloat16)
    reply = lax.dot_general(pick[...], smooth, NN, preferred_element_type=jnp.float32).astype(
        jnp.bfloat16
    )
    for dest in range(wide):
        out_ref[dest, :elements, :] = smooth[dest * elements : (dest + 1) * elements, :]
        out_ref[dest, elements:, :] = reply[dest * rows : (dest + 1) * rows, :]


def coarse_stage(arrived, elements, faces):
    wide, rows, span = arrived.shape
    width = span - LANES
    count = wide * elements
    return pl.pallas_call(
        functools.partial(coarse_kernel, faces, elements),
        in_specs=[VECTOR],
        out_specs=VECTOR,
        out_shape=jax.ShapeDtypeStruct((wide, elements + rows, width), jnp.bfloat16),
        scratch_shapes=[
            pltpu.VMEM((wide * rows, count), jnp.bfloat16),
            pltpu.VMEM((count, count), jnp.bfloat16),
            pltpu.VMEM((wide * rows, width), jnp.bfloat16),
        ],
        compiler_params=pltpu.CompilerParams(vmem_limit_bytes=48 * 1024 * 1024),
        cost_estimate=pl.CostEstimate(
            flops=8 * count * wide * rows * width,
            bytes_accessed=4 * wide * rows * width,
            transcendentals=0,
        ),
        name="coarse_stage",
    )(arrived)


def restrict_kernel(shifts, place_ref, fine_ids, inverse_ref, back_ref, *refs):
    tables, heads = refs[:shifts], refs[shifts : 2 * shifts]
    coarse_ref, fine_ref, rows, sums = refs[2 * shifts :]
    wide, targets, width = back_ref.shape
    elements, block, _ = coarse_ref.shape
    fine_count = fine_ref.shape[0]
    across = rows.shape[0]
    for source in range(wide):
        for piece in range(width // LANES):
            row, lane = divmod(source * (width // LANES) + piece, across)
            rows[lane, row * targets : (row + 1) * targets, :] = back_ref[
                source, :, lanes(piece)
            ].astype(jnp.float32)

    def picked(target):
        parts = [rows[lane, pl.ds(target, block, stride=targets), :] for lane in range(across)]
        return jnp.concatenate(parts, axis=1)

    sums[...] = jnp.zeros_like(sums)
    for shift in range(shifts):
        part = place_ref[0] + shift
        part = jnp.where(part >= shifts, part - shifts, part)
        pairs = tables[shift].shape[0]

        def turn(pair):
            start = pair * NB
            if not isinstance(pair, int):
                start = pl.multiple_of(start, NB)
            coefs = picked(elements + shift * pairs + pair)
            parts = transfer(coefs, tables[shift], heads[shift], pair, start, 1)
            fine = fine_ids[part * pairs + pair]
            for lane in range(across):
                sums[fine, :, lanes(lane)] += parts[lane].astype(jnp.bfloat16).astype(jnp.float32)

        if shifts <= 2:
            for pair in range(pairs):
                turn(pair)
        else:
            pl.loop(0, pairs)(turn)
    for element in range(elements):
        coarse_ref[element] = picked(element).astype(jnp.bfloat16)
    for fine in range(fine_count):
        fine_ref[fine] = (inverse_ref[fine] * sums[fine]).astype(jnp.bfloat16)


def restrict(place, fine_ids, inverse, back, tables, heads, elements, block):
    pairs, _, _, quad = tables[0].shape
    fine_count = inverse.shape[0]
    targets = back.shape[1]
    basis = NB * NB * NB
    return pl.pallas_call(
        functools.partial(restrict_kernel, len(tables)),
        in_specs=[SCALAR] * 3 + [VECTOR] * (1 + 2 * len(tables)),
        out_specs=[VECTOR, VECTOR],
        out_shape=[
            jax.ShapeDtypeStruct((elements, block, basis), jnp.bfloat16),
            jax.ShapeDtypeStruct((fine_count, block, basis), jnp.bfloat16),
        ],
        scratch_shapes=[
            pltpu.VMEM((basis // LANES, block * targets, LANES), jnp.float32),
            pltpu.VMEM((fine_count, block, basis), jnp.float32),
        ],
        compiler_params=pltpu.CompilerParams(
            vmem_limit_bytes=(24 if len(tables) <= 2 else 56) * 1024 * 1024
        ),
        cost_estimate=pl.CostEstimate(
            flops=4 * len(tables) * pairs * NB * block * LANES * quad,
            bytes_accessed=2 * len(tables) * pairs * NB * NB * quad,
            transcendentals=0,
        ),
        name="restrict",
    )(place, fine_ids, inverse, back, *tables, *heads)


def shards(
    fine_field_in,
    fine_points,
    coarse_points,
    quad_weights,
    pair_fine,
    pair_owner,
    pair_coarse,
    coarse_faces,
    coarse_inv_mass,
    fine_inv_mass,
):
    nwide = lax.axis_size("wide")
    nfield = lax.axis_size("field")
    place = lax.axis_index("field").astype(jnp.int32).reshape(1)
    block = fine_field_in.shape[1]
    elements, faces = coarse_faces.shape

    own = jnp.concatenate(
        [
            jnp.swapaxes(fine_points, 0, 1),
            jnp.swapaxes(coarse_points, 0, 1),
            quad_weights[None],
        ],
        axis=0,
    )
    points = [own]
    for shift in range(1, nfield):
        perm = [((i + shift) % nfield, i) for i in range(nfield)]
        points.append(lax.ppermute(own, "field", perm))

    scalars = [pair_owner.T, pair_coarse, coarse_faces.T, coarse_inv_mass]
    tables, heads, outs = [], [], []
    for shift in range(nfield):
        table, head, out = project(
            place, pair_fine, scalars, points[shift], fine_field_in, outs, shift, nfield, nwide
        )
        tables.append(table)
        heads.append(head)
        outs.append(out)
    arrived = lax.all_to_all(outs[-1], "wide", split_axis=0, concat_axis=0, tiled=True)
    smooth = coarse_stage(arrived, elements, faces)
    back = lax.all_to_all(smooth, "wide", split_axis=0, concat_axis=0, tiled=True)
    return restrict(place, pair_fine, fine_inv_mass, back, tables, heads, elements, block)


def solution(mesh):
    placed = (
        P("wide", "field", None),
        P(("wide", "field"), None, None),
        P(("wide", "field"), None, None),
        P(("wide", "field"), None),
        P("wide"),
        P("wide", None),
        P("wide"),
        P("wide", None),
        P("wide"),
        P("wide"),
    )
    return jax.shard_map(
        shards,
        mesh=mesh,
        in_specs=placed,
        out_specs=(P("wide", "field", None), P("wide", "field", None)),
        check_vma=False,
    )
```

```python
import functools
import math

import jax
import jax.numpy as jnp
from jax import lax
from jax.experimental import pallas as pl
from jax.experimental.pallas import tpu as pltpu
from jax.sharding import PartitionSpec as P

NB = 8
DIFFUSE = 0.125
LANES = 128
DIGIT = 7

NT = (((1,), (1,)), ((), ()))
NN = (((1,), (0,)), ((), ()))
TN = (((0,), (0,)), ((), ()))

SCALAR = pl.BlockSpec(memory_space=pltpu.SMEM)
VECTOR = pl.BlockSpec(memory_space=pltpu.VMEM)


def legendre(points, count):
    values = [jnp.ones_like(points), points]
    for degree in range(1, count - 1):
        values.append(
            ((2 * degree + 1) / (degree + 1)) * points * values[degree]
            - (degree / (degree + 1)) * values[degree - 1]
        )
    values = values[:count]
    return [values[n] * math.sqrt((2 * n + 1) / 2.0) for n in range(count)]


def lanes(index):
    return slice(index * LANES, (index + 1) * LANES)


def spread(ref, coord, lane, row):
    return jnp.broadcast_to(ref[coord, lane, pl.ds(row, 1), :], (NB, LANES))


def fill_table(table_ref, legs, pair):
    for side in range(2):
        for lane in range(legs.shape[1]):
            third = legs[2 * side + 1, lane, pl.ds(pair * NB, NB), :]
            for b in range(0, NB, 2):
                both = [
                    spread(legs, 2 * side, lane, pair * NB + b + step) * third for step in range(2)
                ]
                table_ref[pair, side, b * NB : (b + 2) * NB, lanes(lane)] = jnp.concatenate(
                    both, axis=0
                ).astype(jnp.bfloat16)


def transfer(coefs, table_ref, heads, pair, row, source):
    block = coefs.shape[0]
    quad = table_ref.shape[3]
    side = lax.broadcasted_iota(jnp.int32, (block, LANES), 1) < NB * NB
    keep = [
        jnp.where(side, 1.0, 0.0).astype(jnp.bfloat16),
        jnp.where(side, 0.0, 1.0).astype(jnp.bfloat16),
    ]
    masked = jnp.concatenate(
        [coefs[:, lanes(a // 2)] * keep[a % 2] for a in range(NB)], axis=0
    )
    total = None
    for start in range(0, quad, 2 * LANES):
        columns = slice(start, start + 2 * LANES)
        inward = table_ref[pair, source, :, columns]
        outward = table_ref[pair, 1 - source, :, columns]
        inner = lax.dot_general(
            masked,
            jnp.concatenate([inward, inward], axis=0),
            NN,
            preferred_element_type=jnp.float32,
        )
        outer = []
        for half in range(2):
            lane = start // LANES + half
            enter = [spread(heads, source, lane, row + a) for a in range(NB)]
            leave = [spread(heads, 1 - source, lane, row + a) for a in range(NB)]
            pieces = [[] for _ in range(NB)]
            for low in range(0, block, NB):
                value = None
                for a in range(NB):
                    part = inner[a * block + low : a * block + low + NB, lanes(half)]
                    part = part * enter[a]
                    value = part if value is None else value + part
                for a in range(NB):
                    pieces[a].append(value * leave[a])
            outer.append(jnp.concatenate([p for piece in pieces for p in piece], axis=0))
        part = lax.dot_general(
            jnp.concatenate(outer, axis=1).astype(jnp.bfloat16),
            jnp.concatenate([outward, outward], axis=0),
            NT,
            preferred_element_type=jnp.float32,
        )
        total = part if total is None else total + part
    return [
        jnp.where(side, total[a * block : (a + 1) * block], total[(a + 1) * block : (a + 2) * block])
        for a in range(0, NB, 2)
    ]


def facts(owner_ref, coarse_ref, faces_ref, inverse_ref, rows, pair_at):
    faces, elements = faces_ref.shape
    lane = lax.broadcasted_iota(jnp.int32, (1, LANES), 1)
    lines = []
    for row in range(rows):
        line = jnp.zeros((1, LANES), jnp.float32)
        if row < coarse_ref.shape[0]:
            pair = pair_at(row)
            line = jnp.where(lane == 0, owner_ref[0, pair].astype(jnp.float32), line)
            line = jnp.where(lane == 1, coarse_ref[pair].astype(jnp.float32), line)
        if row < elements:
            for face in range(faces):
                name = faces_ref[face, row]
                outer = lax.shift_right_logical(name, DIGIT)
                inner = name - lax.shift_left(outer, DIGIT)
                line = jnp.where(lane == 2 + 2 * face, outer.astype(jnp.float32), line)
                line = jnp.where(lane == 3 + 2 * face, inner.astype(jnp.float32), line)
            rest = jnp.full((1, LANES), inverse_ref[row], jnp.float32)
            for part in range(3):
                head = rest.astype(jnp.bfloat16).astype(jnp.float32)
                line = jnp.where(lane == 2 + 2 * faces + part, head, line)
                rest = rest - head
        lines.append(line)
    return jnp.concatenate(lines, axis=0).astype(jnp.bfloat16)


def project_kernel(shift, shifts, place_ref, fine_ref, *refs):
    last = shift == shifts - 1
    refs = list(refs)
    if last:
        owner_ref, coarse_ref, faces_ref, inverse_ref = refs[:4]
        refs = refs[4:]
    points_ref, field_ref = refs[:2]
    before = refs[2:-5]
    table_ref, heads, out_ref, legs, sums = refs[-5:]
    pairs = points_ref.shape[1]
    block = field_ref.shape[1]
    across = sums.shape[0]

    def pair_at(step, pair):
        part = place_ref[0] + step
        return jnp.where(part >= shifts, part - shifts, part) * pairs + pair

    for lane in range(legs.shape[1]):
        for coord in range(6):
            side, axis = divmod(coord, 3)
            values = legendre(points_ref[coord, :, lanes(lane)], NB)
            for n in range(NB):
                rows = pl.ds(n, pairs, stride=NB)
                if axis:
                    legs[2 * side + axis - 1, lane, rows, :] = values[n]
                elif side:
                    heads[side, lane, rows, :] = values[n] * points_ref[6, :, lanes(lane)]
                else:
                    heads[side, lane, rows, :] = values[n]

    for pair in range(pairs):
        fill_table(table_ref, legs, pair)
        coefs = field_ref[fine_ref[pair_at(shift, pair)]]
        parts = transfer(coefs, table_ref, heads, pair, pair * NB, 0)
        for lane in range(across):
            sums[lane, pl.ds(pair, block, stride=pairs), :] = parts[lane]

    if not last:
        out_ref[...] = sums[...]
        return
    wide, total, span = out_ref.shape
    width = span - LANES
    extra = facts(
        owner_ref,
        coarse_ref,
        faces_ref,
        inverse_ref,
        total,
        lambda row: pair_at(row // pairs, row % pairs),
    )
    sources = list(before) + [sums]
    for dest in range(wide):
        for piece in range(width // LANES):
            row, lane = divmod(dest * (width // LANES) + piece, across)
            parts = [s[lane, row * pairs : (row + 1) * pairs, :] for s in sources]
            out_ref[dest, :, lanes(piece)] = jnp.concatenate(parts, axis=0).astype(jnp.bfloat16)
        out_ref[dest, :, lanes(width // LANES)] = extra


def project(place, fine_ids, scalars, points, field, before, shift, shifts, wide):
    _, pairs, quad = points.shape
    _, block, basis = field.shape
    last = shift == shifts - 1
    across = basis // LANES
    operands = [place, fine_ids] + (scalars if last else [])
    vectors = [points, field] + (before if last else [])
    if last:
        out = jax.ShapeDtypeStruct(
            (wide, shifts * pairs, block * basis // wide + LANES), jnp.bfloat16
        )
    else:
        out = jax.ShapeDtypeStruct((across, block * pairs, LANES), jnp.float32)
    return pl.pallas_call(
        functools.partial(project_kernel, shift, shifts),
        in_specs=[SCALAR] * len(operands) + [VECTOR] * len(vectors),
        out_specs=[VECTOR] * 3,
        out_shape=[
            jax.ShapeDtypeStruct((pairs, 2, NB * NB, quad), jnp.bfloat16),
            jax.ShapeDtypeStruct((2, quad // LANES, pairs * NB, LANES), jnp.float32),
            out,
        ],
        scratch_shapes=[
            pltpu.VMEM((4, quad // LANES, pairs * NB, LANES), jnp.float32),
            pltpu.VMEM((across, block * pairs, LANES), jnp.float32),
        ],
        compiler_params=pltpu.CompilerParams(vmem_limit_bytes=24 * 1024 * 1024),
        cost_estimate=pl.CostEstimate(
            flops=4 * pairs * NB * block * LANES * quad,
            bytes_accessed=2 * pairs * NB * NB * quad,
            transcendentals=0,
        ),
        name="project",
    )(*operands, *vectors)


def coarse_kernel(faces, elements, arrived_ref, out_ref, pick, near, moved):
    wide, rows, span = arrived_ref.shape
    width = span - LANES
    count = wide * elements
    name = lax.broadcasted_iota(jnp.int32, (rows, count), 1).astype(jnp.float32)
    inverse = []
    for source in range(wide):
        fact = arrived_ref[source, :, width:].astype(jnp.float32)
        moved[source * rows : (source + 1) * rows, :] = arrived_ref[source, :, :width]
        index = fact[:, 0:1] * elements + fact[:, 1:2]
        pick[source * rows : (source + 1) * rows, :] = (index == name).astype(jnp.float32).astype(
            jnp.bfloat16
        )
        hits = jnp.zeros((elements, count), jnp.float32)
        for face in range(faces):
            index = fact[:elements, 2 + 2 * face : 3 + 2 * face] * float(1 << DIGIT)
            index = index + fact[:elements, 3 + 2 * face : 4 + 2 * face]
            hits = hits + (index == name[:elements]).astype(jnp.float32)
        near[source * elements : (source + 1) * elements, :] = hits.astype(jnp.bfloat16)
        first = 2 + 2 * faces
        inverse.append(
            fact[:elements, first : first + 1]
            + fact[:elements, first + 1 : first + 2]
            + fact[:elements, first + 2 : first + 3]
        )
    load = lax.dot_general(pick[...], moved[...], TN, preferred_element_type=jnp.float32)
    solved = jnp.concatenate(inverse, axis=0) * load
    high = solved.astype(jnp.bfloat16)
    low = (solved - high.astype(jnp.float32)).astype(jnp.bfloat16)
    beside = lax.dot_general(near[...], high, NN, preferred_element_type=jnp.float32)
    beside = beside + lax.dot_general(near[...], low, NN, preferred_element_type=jnp.float32)
    smooth = (solved + DIFFUSE * (beside - float(faces) * solved)).astype(jnp.bfloat16)
    reply = lax.dot_general(pick[...], smooth, NN, preferred_element_type=jnp.float32).astype(
        jnp.bfloat16
    )
    for dest in range(wide):
        out_ref[dest, :elements, :] = smooth[dest * elements : (dest + 1) * elements, :]
        out_ref[dest, elements:, :] = reply[dest * rows : (dest + 1) * rows, :]


def coarse_stage(arrived, elements, faces):
    wide, rows, span = arrived.shape
    width = span - LANES
    count = wide * elements
    return pl.pallas_call(
        functools.partial(coarse_kernel, faces, elements),
        in_specs=[VECTOR],
        out_specs=VECTOR,
        out_shape=jax.ShapeDtypeStruct((wide, elements + rows, width), jnp.bfloat16),
        scratch_shapes=[
            pltpu.VMEM((wide * rows, count), jnp.bfloat16),
            pltpu.VMEM((count, count), jnp.bfloat16),
            pltpu.VMEM((wide * rows, width), jnp.bfloat16),
        ],
        compiler_params=pltpu.CompilerParams(vmem_limit_bytes=48 * 1024 * 1024),
        cost_estimate=pl.CostEstimate(
            flops=8 * count * wide * rows * width,
            bytes_accessed=4 * wide * rows * width,
            transcendentals=0,
        ),
        name="coarse_stage",
    )(arrived)


def restrict_kernel(shifts, place_ref, fine_ids, inverse_ref, back_ref, *refs):
    tables, heads = refs[:shifts], refs[shifts : 2 * shifts]
    coarse_ref, fine_ref, rows, sums = refs[2 * shifts :]
    wide, targets, width = back_ref.shape
    elements, block, _ = coarse_ref.shape
    fine_count = fine_ref.shape[0]
    across = rows.shape[0]
    for source in range(wide):
        for piece in range(width // LANES):
            row, lane = divmod(source * (width // LANES) + piece, across)
            rows[lane, row * targets : (row + 1) * targets, :] = back_ref[
                source, :, lanes(piece)
            ].astype(jnp.float32)

    def picked(target):
        parts = [rows[lane, pl.ds(target, block, stride=targets), :] for lane in range(across)]
        return jnp.concatenate(parts, axis=1).astype(jnp.bfloat16)

    sums[...] = jnp.zeros_like(sums)
    for shift in range(shifts):
        part = place_ref[0] + shift
        part = jnp.where(part >= shifts, part - shifts, part)
        pairs = tables[shift].shape[0]

        def turn(pair):
            start = pair * NB
            if not isinstance(pair, int):
                start = pl.multiple_of(start, NB)
            coefs = picked(elements + shift * pairs + pair)
            parts = transfer(coefs, tables[shift], heads[shift], pair, start, 1)
            fine = fine_ids[part * pairs + pair]
            for lane in range(across):
                sums[fine, :, lanes(lane)] += parts[lane].astype(jnp.bfloat16).astype(jnp.float32)

        if shifts <= 2:
            for pair in range(pairs):
                turn(pair)
        else:
            pl.loop(0, pairs)(turn)
    for element in range(elements):
        coarse_ref[element] = picked(element)
    for fine in range(fine_count):
        fine_ref[fine] = (inverse_ref[fine] * sums[fine]).astype(jnp.bfloat16)


def restrict(place, fine_ids, inverse, back, tables, heads, elements, block):
    pairs, _, _, quad = tables[0].shape
    fine_count = inverse.shape[0]
    targets = back.shape[1]
    basis = NB * NB * NB
    return pl.pallas_call(
        functools.partial(restrict_kernel, len(tables)),
        in_specs=[SCALAR] * 3 + [VECTOR] * (1 + 2 * len(tables)),
        out_specs=[VECTOR, VECTOR],
        out_shape=[
            jax.ShapeDtypeStruct((elements, block, basis), jnp.bfloat16),
            jax.ShapeDtypeStruct((fine_count, block, basis), jnp.bfloat16),
        ],
        scratch_shapes=[
            pltpu.VMEM((basis // LANES, block * targets, LANES), jnp.float32),
            pltpu.VMEM((fine_count, block, basis), jnp.float32),
        ],
        compiler_params=pltpu.CompilerParams(
            vmem_limit_bytes=(24 if len(tables) <= 2 else 56) * 1024 * 1024
        ),
        cost_estimate=pl.CostEstimate(
            flops=4 * len(tables) * pairs * NB * block * LANES * quad,
            bytes_accessed=2 * len(tables) * pairs * NB * NB * quad,
            transcendentals=0,
        ),
        name="restrict",
    )(place, fine_ids, inverse, back, *tables, *heads)


def shards(
    fine_field_in,
    fine_points,
    coarse_points,
    quad_weights,
    pair_fine,
    pair_owner,
    pair_coarse,
    coarse_faces,
    coarse_inv_mass,
    fine_inv_mass,
):
    nwide = lax.axis_size("wide")
    nfield = lax.axis_size("field")
    place = lax.axis_index("field").astype(jnp.int32).reshape(1)
    block = fine_field_in.shape[1]
    elements, faces = coarse_faces.shape

    own = jnp.concatenate(
        [
            jnp.swapaxes(fine_points, 0, 1),
            jnp.swapaxes(coarse_points, 0, 1),
            quad_weights[None],
        ],
        axis=0,
    )
    points = [own]
    for shift in range(1, nfield):
        perm = [((i + shift) % nfield, i) for i in range(nfield)]
        points.append(lax.ppermute(own, "field", perm))

    scalars = [pair_owner.T, pair_coarse, coarse_faces.T, coarse_inv_mass]
    tables, heads, outs = [], [], []
    for shift in range(nfield):
        table, head, out = project(
            place, pair_fine, scalars, points[shift], fine_field_in, outs, shift, nfield, nwide
        )
        tables.append(table)
        heads.append(head)
        outs.append(out)
    arrived = lax.all_to_all(outs[-1], "wide", split_axis=0, concat_axis=0, tiled=True)
    smooth = coarse_stage(arrived, elements, faces)
    back = lax.all_to_all(smooth, "wide", split_axis=0, concat_axis=0, tiled=True)
    return restrict(place, pair_fine, fine_inv_mass, back, tables, heads, elements, block)


def solution(mesh):
    placed = (
        P("wide", "field", None),
        P(("wide", "field"), None, None),
        P(("wide", "field"), None, None),
        P(("wide", "field"), None),
        P("wide"),
        P("wide", None),
        P("wide"),
        P("wide", None),
        P("wide"),
        P("wide"),
    )
    return jax.shard_map(
        shards,
        mesh=mesh,
        in_specs=placed,
        out_specs=(P("wide", "field", None), P("wide", "field", None)),
        check_vma=False,
    )
```

```python
import functools
import math

import jax
import jax.numpy as jnp
from jax import lax
from jax.experimental import pallas as pl
from jax.experimental.pallas import tpu as pltpu
from jax.sharding import PartitionSpec as P

NB = 8
DIFFUSE = 0.125
LANES = 128
DIGIT = 7
SPAN = 4

NT = (((1,), (1,)), ((), ()))
NN = (((1,), (0,)), ((), ()))
TN = (((0,), (0,)), ((), ()))

SCALAR = pl.BlockSpec(memory_space=pltpu.SMEM)
VECTOR = pl.BlockSpec(memory_space=pltpu.VMEM)


def legendre(points, count):
    values = [jnp.ones_like(points), points]
    for degree in range(1, count - 1):
        values.append(
            ((2 * degree + 1) / (degree + 1)) * points * values[degree]
            - (degree / (degree + 1)) * values[degree - 1]
        )
    values = values[:count]
    return [values[n] * math.sqrt((2 * n + 1) / 2.0) for n in range(count)]


def lanes(index):
    return slice(index * LANES, (index + 1) * LANES)


def spread(ref, coord, lane, row):
    return jnp.broadcast_to(ref[coord, lane, pl.ds(row, 1), :], (NB, LANES))


def fill_table(table_ref, legs, pair):
    for side in range(2):
        for lane in range(legs.shape[1]):
            third = legs[2 * side + 1, lane, pl.ds(pair * NB, NB), :]
            for b in range(0, NB, 2):
                both = [
                    spread(legs, 2 * side, lane, pair * NB + b + step) * third for step in range(2)
                ]
                table_ref[pair, side, b * NB : (b + 2) * NB, lanes(lane)] = jnp.concatenate(
                    both, axis=0
                ).astype(jnp.bfloat16)


def transfer(coefs, table_ref, heads, pair, row, source):
    block = coefs.shape[0]
    quad = table_ref.shape[3]
    side = lax.broadcasted_iota(jnp.int32, (block, LANES), 1) < NB * NB
    keep = [
        jnp.where(side, 1.0, 0.0).astype(jnp.bfloat16),
        jnp.where(side, 0.0, 1.0).astype(jnp.bfloat16),
    ]
    masked = jnp.concatenate(
        [coefs[:, lanes(a // 2)] * keep[a % 2] for a in range(NB)], axis=0
    )
    total = None
    for start in range(0, quad, SPAN * LANES):
        columns = slice(start, start + SPAN * LANES)
        inward = table_ref[pair, source, :, columns]
        outward = table_ref[pair, 1 - source, :, columns]
        inner = lax.dot_general(
            masked,
            jnp.concatenate([inward, inward], axis=0),
            NN,
            preferred_element_type=jnp.float32,
        )
        outer = []
        for half in range(SPAN):
            lane = start // LANES + half
            enter = [spread(heads, source, lane, row + a) for a in range(NB)]
            leave = [spread(heads, 1 - source, lane, row + a) for a in range(NB)]
            pieces = [[] for _ in range(NB)]
            for low in range(0, block, NB):
                value = None
                for a in range(NB):
                    part = inner[a * block + low : a * block + low + NB, lanes(half)]
                    part = part * enter[a]
                    value = part if value is None else value + part
                for a in range(NB):
                    pieces[a].append(value * leave[a])
            outer.append(jnp.concatenate([p for piece in pieces for p in piece], axis=0))
        part = lax.dot_general(
            jnp.concatenate(outer, axis=1).astype(jnp.bfloat16),
            jnp.concatenate([outward, outward], axis=0),
            NT,
            preferred_element_type=jnp.float32,
        )
        total = part if total is None else total + part
    return [
        jnp.where(side, total[a * block : (a + 1) * block], total[(a + 1) * block : (a + 2) * block])
        for a in range(0, NB, 2)
    ]


def facts(owner_ref, coarse_ref, faces_ref, inverse_ref, rows, pair_at):
    faces, elements = faces_ref.shape
    lane = lax.broadcasted_iota(jnp.int32, (1, LANES), 1)
    lines = []
    for row in range(rows):
        line = jnp.zeros((1, LANES), jnp.float32)
        if row < coarse_ref.shape[0]:
            pair = pair_at(row)
            line = jnp.where(lane == 0, owner_ref[0, pair].astype(jnp.float32), line)
            line = jnp.where(lane == 1, coarse_ref[pair].astype(jnp.float32), line)
        if row < elements:
            for face in range(faces):
                name = faces_ref[face, row]
                outer = lax.shift_right_logical(name, DIGIT)
                inner = name - lax.shift_left(outer, DIGIT)
                line = jnp.where(lane == 2 + 2 * face, outer.astype(jnp.float32), line)
                line = jnp.where(lane == 3 + 2 * face, inner.astype(jnp.float32), line)
            rest = jnp.full((1, LANES), inverse_ref[row], jnp.float32)
            for part in range(3):
                head = rest.astype(jnp.bfloat16).astype(jnp.float32)
                line = jnp.where(lane == 2 + 2 * faces + part, head, line)
                rest = rest - head
        lines.append(line)
    return jnp.concatenate(lines, axis=0).astype(jnp.bfloat16)


def project_kernel(shift, shifts, place_ref, fine_ref, *refs):
    last = shift == shifts - 1
    refs = list(refs)
    if last:
        owner_ref, coarse_ref, faces_ref, inverse_ref = refs[:4]
        refs = refs[4:]
    points_ref, field_ref = refs[:2]
    before = refs[2:-5]
    table_ref, heads, out_ref, legs, sums = refs[-5:]
    pairs = points_ref.shape[1]
    block = field_ref.shape[1]
    across = sums.shape[0]

    def pair_at(step, pair):
        part = place_ref[0] + step
        return jnp.where(part >= shifts, part - shifts, part) * pairs + pair

    for lane in range(legs.shape[1]):
        for coord in range(6):
            side, axis = divmod(coord, 3)
            values = legendre(points_ref[coord, :, lanes(lane)], NB)
            for n in range(NB):
                rows = pl.ds(n, pairs, stride=NB)
                if axis:
                    legs[2 * side + axis - 1, lane, rows, :] = values[n]
                elif side:
                    heads[side, lane, rows, :] = values[n] * points_ref[6, :, lanes(lane)]
                else:
                    heads[side, lane, rows, :] = values[n]

    for pair in range(pairs):
        fill_table(table_ref, legs, pair)
        coefs = field_ref[fine_ref[pair_at(shift, pair)]]
        parts = transfer(coefs, table_ref, heads, pair, pair * NB, 0)
        for lane in range(across):
            sums[lane, pl.ds(pair, block, stride=pairs), :] = parts[lane]

    if not last:
        out_ref[...] = sums[...]
        return
    wide, total, span = out_ref.shape
    width = span - LANES
    extra = facts(
        owner_ref,
        coarse_ref,
        faces_ref,
        inverse_ref,
        total,
        lambda row: pair_at(row // pairs, row % pairs),
    )
    sources = list(before) + [sums]
    for dest in range(wide):
        for piece in range(width // LANES):
            row, lane = divmod(dest * (width // LANES) + piece, across)
            parts = [s[lane, row * pairs : (row + 1) * pairs, :] for s in sources]
            out_ref[dest, :, lanes(piece)] = jnp.concatenate(parts, axis=0).astype(jnp.bfloat16)
        out_ref[dest, :, lanes(width // LANES)] = extra


def project(place, fine_ids, scalars, points, field, before, shift, shifts, wide):
    _, pairs, quad = points.shape
    _, block, basis = field.shape
    last = shift == shifts - 1
    across = basis // LANES
    operands = [place, fine_ids] + (scalars if last else [])
    vectors = [points, field] + (before if last else [])
    if last:
        out = jax.ShapeDtypeStruct(
            (wide, shifts * pairs, block * basis // wide + LANES), jnp.bfloat16
        )
    else:
        out = jax.ShapeDtypeStruct((across, block * pairs, LANES), jnp.float32)
    return pl.pallas_call(
        functools.partial(project_kernel, shift, shifts),
        in_specs=[SCALAR] * len(operands) + [VECTOR] * len(vectors),
        out_specs=[VECTOR] * 3,
        out_shape=[
            jax.ShapeDtypeStruct((pairs, 2, NB * NB, quad), jnp.bfloat16),
            jax.ShapeDtypeStruct((2, quad // LANES, pairs * NB, LANES), jnp.float32),
            out,
        ],
        scratch_shapes=[
            pltpu.VMEM((4, quad // LANES, pairs * NB, LANES), jnp.float32),
            pltpu.VMEM((across, block * pairs, LANES), jnp.float32),
        ],
        compiler_params=pltpu.CompilerParams(vmem_limit_bytes=24 * 1024 * 1024),
        cost_estimate=pl.CostEstimate(
            flops=4 * pairs * NB * block * LANES * quad,
            bytes_accessed=2 * pairs * NB * NB * quad,
            transcendentals=0,
        ),
        name="project",
    )(*operands, *vectors)


def coarse_kernel(faces, elements, arrived_ref, out_ref, pick, near, moved):
    wide, rows, span = arrived_ref.shape
    width = span - LANES
    count = wide * elements
    name = lax.broadcasted_iota(jnp.int32, (rows, count), 1).astype(jnp.float32)
    inverse = []
    for source in range(wide):
        fact = arrived_ref[source, :, width:].astype(jnp.float32)
        moved[source * rows : (source + 1) * rows, :] = arrived_ref[source, :, :width]
        index = fact[:, 0:1] * elements + fact[:, 1:2]
        pick[source * rows : (source + 1) * rows, :] = (index == name).astype(jnp.float32).astype(
            jnp.bfloat16
        )
        hits = jnp.zeros((elements, count), jnp.float32)
        for face in range(faces):
            index = fact[:elements, 2 + 2 * face : 3 + 2 * face] * float(1 << DIGIT)
            index = index + fact[:elements, 3 + 2 * face : 4 + 2 * face]
            hits = hits + (index == name[:elements]).astype(jnp.float32)
        near[source * elements : (source + 1) * elements, :] = hits.astype(jnp.bfloat16)
        first = 2 + 2 * faces
        inverse.append(
            fact[:elements, first : first + 1]
            + fact[:elements, first + 1 : first + 2]
            + fact[:elements, first + 2 : first + 3]
        )
    load = lax.dot_general(pick[...], moved[...], TN, preferred_element_type=jnp.float32)
    solved = jnp.concatenate(inverse, axis=0) * load
    high = solved.astype(jnp.bfloat16)
    low = (solved - high.astype(jnp.float32)).astype(jnp.bfloat16)
    beside = lax.dot_general(near[...], high, NN, preferred_element_type=jnp.float32)
    beside = beside + lax.dot_general(near[...], low, NN, preferred_element_type=jnp.float32)
    smooth = (solved + DIFFUSE * (beside - float(faces) * solved)).astype(jnp.bfloat16)
    reply = lax.dot_general(pick[...], smooth, NN, preferred_element_type=jnp.float32).astype(
        jnp.bfloat16
    )
    for dest in range(wide):
        out_ref[dest, :elements, :] = smooth[dest * elements : (dest + 1) * elements, :]
        out_ref[dest, elements:, :] = reply[dest * rows : (dest + 1) * rows, :]


def coarse_stage(arrived, elements, faces):
    wide, rows, span = arrived.shape
    width = span - LANES
    count = wide * elements
    return pl.pallas_call(
        functools.partial(coarse_kernel, faces, elements),
        in_specs=[VECTOR],
        out_specs=VECTOR,
        out_shape=jax.ShapeDtypeStruct((wide, elements + rows, width), jnp.bfloat16),
        scratch_shapes=[
            pltpu.VMEM((wide * rows, count), jnp.bfloat16),
            pltpu.VMEM((count, count), jnp.bfloat16),
            pltpu.VMEM((wide * rows, width), jnp.bfloat16),
        ],
        compiler_params=pltpu.CompilerParams(vmem_limit_bytes=48 * 1024 * 1024),
        cost_estimate=pl.CostEstimate(
            flops=8 * count * wide * rows * width,
            bytes_accessed=4 * wide * rows * width,
            transcendentals=0,
        ),
        name="coarse_stage",
    )(arrived)


def restrict_kernel(shifts, place_ref, fine_ids, inverse_ref, back_ref, *refs):
    tables, heads = refs[:shifts], refs[shifts : 2 * shifts]
    coarse_ref, fine_ref, rows, sums = refs[2 * shifts :]
    wide, targets, width = back_ref.shape
    elements, block, _ = coarse_ref.shape
    fine_count = fine_ref.shape[0]
    across = rows.shape[0]
    for source in range(wide):
        for piece in range(width // LANES):
            row, lane = divmod(source * (width // LANES) + piece, across)
            rows[lane, row * targets : (row + 1) * targets, :] = back_ref[
                source, :, lanes(piece)
            ].astype(jnp.float32)

    def picked(target):
        parts = [rows[lane, pl.ds(target, block, stride=targets), :] for lane in range(across)]
        return jnp.concatenate(parts, axis=1).astype(jnp.bfloat16)

    sums[...] = jnp.zeros_like(sums)
    for shift in range(shifts):
        part = place_ref[0] + shift
        part = jnp.where(part >= shifts, part - shifts, part)
        pairs = tables[shift].shape[0]

        def turn(pair):
            start = pair * NB
            if not isinstance(pair, int):
                start = pl.multiple_of(start, NB)
            coefs = picked(elements + shift * pairs + pair)
            parts = transfer(coefs, tables[shift], heads[shift], pair, start, 1)
            fine = fine_ids[part * pairs + pair]
            for lane in range(across):
                sums[fine, :, lanes(lane)] += parts[lane].astype(jnp.bfloat16).astype(jnp.float32)

        if shifts <= 2:
            for pair in range(pairs):
                turn(pair)
        else:
            pl.loop(0, pairs)(turn)
    for element in range(elements):
        coarse_ref[element] = picked(element)
    for fine in range(fine_count):
        fine_ref[fine] = (inverse_ref[fine] * sums[fine]).astype(jnp.bfloat16)


def restrict(place, fine_ids, inverse, back, tables, heads, elements, block):
    pairs, _, _, quad = tables[0].shape
    fine_count = inverse.shape[0]
    targets = back.shape[1]
    basis = NB * NB * NB
    return pl.pallas_call(
        functools.partial(restrict_kernel, len(tables)),
        in_specs=[SCALAR] * 3 + [VECTOR] * (1 + 2 * len(tables)),
        out_specs=[VECTOR, VECTOR],
        out_shape=[
            jax.ShapeDtypeStruct((elements, block, basis), jnp.bfloat16),
            jax.ShapeDtypeStruct((fine_count, block, basis), jnp.bfloat16),
        ],
        scratch_shapes=[
            pltpu.VMEM((basis // LANES, block * targets, LANES), jnp.float32),
            pltpu.VMEM((fine_count, block, basis), jnp.float32),
        ],
        compiler_params=pltpu.CompilerParams(
            vmem_limit_bytes=(24 if len(tables) <= 2 else 56) * 1024 * 1024
        ),
        cost_estimate=pl.CostEstimate(
            flops=4 * len(tables) * pairs * NB * block * LANES * quad,
            bytes_accessed=2 * len(tables) * pairs * NB * NB * quad,
            transcendentals=0,
        ),
        name="restrict",
    )(place, fine_ids, inverse, back, *tables, *heads)


def shards(
    fine_field_in,
    fine_points,
    coarse_points,
    quad_weights,
    pair_fine,
    pair_owner,
    pair_coarse,
    coarse_faces,
    coarse_inv_mass,
    fine_inv_mass,
):
    nwide = lax.axis_size("wide")
    nfield = lax.axis_size("field")
    place = lax.axis_index("field").astype(jnp.int32).reshape(1)
    block = fine_field_in.shape[1]
    elements, faces = coarse_faces.shape

    own = jnp.concatenate(
        [
            jnp.swapaxes(fine_points, 0, 1),
            jnp.swapaxes(coarse_points, 0, 1),
            quad_weights[None],
        ],
        axis=0,
    )
    points = [own]
    for shift in range(1, nfield):
        perm = [((i + shift) % nfield, i) for i in range(nfield)]
        points.append(lax.ppermute(own, "field", perm))

    scalars = [pair_owner.T, pair_coarse, coarse_faces.T, coarse_inv_mass]
    tables, heads, outs = [], [], []
    for shift in range(nfield):
        table, head, out = project(
            place, pair_fine, scalars, points[shift], fine_field_in, outs, shift, nfield, nwide
        )
        tables.append(table)
        heads.append(head)
        outs.append(out)
    arrived = lax.all_to_all(outs[-1], "wide", split_axis=0, concat_axis=0, tiled=True)
    smooth = coarse_stage(arrived, elements, faces)
    back = lax.all_to_all(smooth, "wide", split_axis=0, concat_axis=0, tiled=True)
    return restrict(place, pair_fine, fine_inv_mass, back, tables, heads, elements, block)


def solution(mesh):
    placed = (
        P("wide", "field", None),
        P(("wide", "field"), None, None),
        P(("wide", "field"), None, None),
        P(("wide", "field"), None),
        P("wide"),
        P("wide", None),
        P("wide"),
        P("wide", None),
        P("wide"),
        P("wide"),
    )
    return jax.shard_map(
        shards,
        mesh=mesh,
        in_specs=placed,
        out_specs=(P("wide", "field", None), P("wide", "field", None)),
        check_vma=False,
    )
```
